128 devices in a mesh: group: 2 (over y_hi), blk: 64 (over z, y_lo, x, core).
Axes of the slice: x: 4, y: 4 (y_hi: 2, y_lo: 2; y = y_hi * 2 + y_lo), z: 4, core: 2. Of those that a mesh axis runs over, the one named last changes fastest.
Arguments:
- image_features: bfloat16 [98304, 1280], P(('group', 'blk')), may hold values from -1100 to 1100
- text_features: bfloat16 [98304, 1280], P(('group', 'blk')), may hold values from -1100 to 1100
- logit_scale: float32 [1], replicated, may hold values from 30 to 400
- pair_ids: int32 [98304], P(('group', 'blk')), may hold values from 0 to 98303, as said below
Outputs:
- row_gap: float32 [98304], P(('group', 'blk'))
- col_gap: float32 [98304], P(('group', 'blk'))
The draws below stay inside these ranges and needn't reach their ends.
Inputs may be any that keep to these rules, and one draw needn't show every extreme that they name: pair_ids is a permutation of the rows in which pair_ids[i] lies in the same aligned block of 768 rows as i.
All inputs are finite; a program needn't handle non-finite values.
Results may differ from the reference program's by a relative error of at most 0.00091.
Values may be sent and summed in bfloat16 or wider, within the bound.
A program may use at most 64 MiB of HBM per device.

```python
import math
import jax
import jax.numpy as jnp
from jax import lax

D = 1280
ROWS = 768
SHIFTS = 4
BATCH = 98304
N_GROUP = 2
N_BLK = 64


def paired_features(key):
    keys = jax.random.split(key, 11)
    blocks = BATCH // ROWS
    width = min(8, ROWS // 8)
    text_base = jax.random.truncated_normal(keys[0], -5.0, 5.0, (blocks, ROWS, D), jnp.float32)
    image_base = jax.random.truncated_normal(keys[1], -5.0, 5.0, (blocks, ROWS, D), jnp.float32)
    text_rows = jnp.exp(jax.random.uniform(keys[2], (blocks, ROWS, 1), jnp.float32, 0.0, math.log(10.0)))
    image_rows = jnp.exp(jax.random.uniform(keys[3], (blocks, ROWS, 1), jnp.float32, 0.0, math.log(10.0)))
    text_cols = jnp.exp(jax.random.uniform(keys[4], (D,), jnp.float32, 0.0, math.log(10.0)))
    image_cols = jnp.exp(jax.random.uniform(keys[5], (D,), jnp.float32, 0.0, math.log(10.0)))
    noise_ahead = jax.random.truncated_normal(keys[9], -5.0, 5.0, (blocks, width, D), jnp.float32)
    noise_across = jax.random.truncated_normal(keys[10], -5.0, 5.0, (blocks, width, D), jnp.float32)
    grid = image_base.reshape(N_GROUP, N_BLK, ROWS, D)
    ahead = jnp.roll(grid, -SHIFTS, axis=1)[:, :, 2 * width:3 * width].reshape(blocks, width, D)
    across = jnp.roll(jnp.roll(grid, -1, axis=0), -1, axis=1)[:, :, 3 * width:4 * width].reshape(blocks, width, D)
    ahead_text = (ahead + 0.12 * noise_ahead) * image_cols * text_rows[:, 2 * width:3 * width]
    across_text = (across + 0.12 * noise_across) * image_cols * text_rows[:, 3 * width:4 * width]
    text = text_base * text_rows * text_cols
    image = image_base * image_rows * image_cols
    text = text.at[:, width:2 * width].set(text[:, width:2 * width])
    text = text.at[:, 2 * width:3 * width].set(ahead_text)
    text = text.at[:, 3 * width:4 * width].set(across_text)
    image = image.at[:, 0:width].set(image[:, 0:width])
    image = image.at[:, width:2 * width].set(image[:, width:2 * width])
    return (image.reshape(BATCH, D), text.reshape(BATCH, D))


def draw_image_features(key, part):
    image, text = paired_features(key)
    return image.astype(jnp.bfloat16)


def draw_text_features(key, part):
    image, text = paired_features(key)
    return text.astype(jnp.bfloat16)


def draw_logit_scale(key, part):
    key = jax.random.fold_in(key, 5)
    value = jax.random.uniform(key, (1,), jnp.float32, 30.0, 100.0)
    return value


def draw_pair_ids(key, part):
    key = jax.random.fold_in(key, 7)
    blocks = BATCH // ROWS
    keys = jax.random.split(key, blocks)
    perms = jax.vmap(lambda single: jax.random.permutation(single, ROWS))(keys)
    starts = jnp.arange(blocks, dtype=jnp.int32)[:, None] * ROWS
    return (perms.astype(jnp.int32) + starts).reshape(BATCH).astype(jnp.int32)


def setup_inputs(seed: int = 0) -> dict:
    splits = jax.random.split(jax.random.key(seed), 5)
    image_features = draw_image_features(jax.random.fold_in(splits[4], 71), 0)
    text_features = draw_text_features(jax.random.fold_in(splits[4], 71), 0)
    logit_scale = draw_logit_scale(jax.random.fold_in(splits[4], 71), 0)
    pair_ids = draw_pair_ids(jax.random.fold_in(splits[4], 71), 0)
    return {"image_features": image_features, "text_features": text_features, "logit_scale": logit_scale, "pair_ids": pair_ids}


def unit_rows(features):
    wide = features.astype(jnp.float32)
    inverse = lax.rsqrt(lax.optimization_barrier(jnp.mean(wide * wide, axis=-1, keepdims=True)) + 1e-06)
    return (wide * inverse * features.shape[-1] ** (-0.5)).astype(jnp.bfloat16)

def reference(image_features, text_features, logit_scale, pair_ids):
    blocks = N_GROUP * N_BLK
    image_unit = unit_rows(image_features).reshape(blocks, ROWS, D)
    text_unit = unit_rows(text_features).reshape(blocks, ROWS, D)
    pair_blocks = pair_ids.reshape(blocks, ROWS)
    scale = logit_scale[0].astype(jnp.float32)
    offsets = jnp.arange(SHIFTS + 1, dtype=jnp.int32)

    def one_block(index):
        group_index = index // N_BLK
        blk_index = index % N_BLK
        cycle_index = (blk_index - offsets) % N_BLK
        own_ids = group_index * N_BLK + cycle_index
        other_ids = (group_index - 1) % N_GROUP * N_BLK + cycle_index
        window = text_unit[jnp.concatenate([own_ids, other_ids]).astype(jnp.int32)]
        scores = scale * jnp.einsum('rd,wcd->rwc', image_unit[index].astype(jnp.float32), window.astype(jnp.float32))
        flat = scores.reshape(ROWS, -1)
        row_top = lax.optimization_barrier(jnp.max(flat, axis=1))
        row_lse = row_top + jnp.log(lax.optimization_barrier(jnp.sum(jnp.exp(flat - row_top[:, None]), axis=1)))
        col_top = lax.optimization_barrier(jnp.max(scores, axis=0))
        col_total = lax.optimization_barrier(jnp.sum(jnp.exp(scores - col_top[None]), axis=0))
        local = (pair_blocks[index] % ROWS).astype(jnp.int32)
        positive = jnp.take_along_axis(scores[:, 0, :], local[:, None], axis=1)[:, 0]
        col_positive = jnp.zeros((ROWS,), scores.dtype).at[local].set(positive)
        return (row_lse - positive, col_top, col_total, col_positive)
    row_gap, col_top, col_total, col_positive = lax.map(one_block, jnp.arange(blocks, dtype=jnp.int32))
    col_top = col_top.reshape(N_GROUP, N_BLK, 2, SHIFTS + 1, ROWS)
    col_total = col_total.reshape(N_GROUP, N_BLK, 2, SHIFTS + 1, ROWS)
    tops = []
    totals = []
    for shift in range(SHIFTS + 1):
        tops.append(jnp.roll(col_top[:, :, 0, shift], -shift, axis=1))
        totals.append(jnp.roll(col_total[:, :, 0, shift], -shift, axis=1))
        tops.append(jnp.roll(jnp.roll(col_top[:, :, 1, shift], -shift, axis=1), -1, axis=0))
        totals.append(jnp.roll(jnp.roll(col_total[:, :, 1, shift], -shift, axis=1), -1, axis=0))
    tops = jnp.stack(tops)
    totals = jnp.stack(totals)
    highest = lax.optimization_barrier(jnp.max(tops, axis=0))
    summed = lax.optimization_barrier(jnp.sum(totals * jnp.exp(tops - highest[None]), axis=0))
    col_gap = (highest + jnp.log(summed)).reshape(BATCH) - col_positive.reshape(BATCH)
    return (row_gap.reshape(BATCH), col_gap)
```

```python
import math

import jax
import jax.numpy as jnp
from jax import lax
from jax.experimental import pallas as pl
from jax.experimental.pallas import tpu as pltpu
from jax.sharding import PartitionSpec as P

MESH = pl.DeviceIdType.MESH
ROWS = 768
D = 1280
NBLK = 64
Q = 128
NQ = ROWS // Q
NA = 2
MI = 384
NT = 256
LOG2E = math.log2(math.e)
LN2 = math.log(2.0)
LOW = -1e30

K_I, K_A, K_C, K_O, K_A2, K_B, K_R, K_R2, K_R2B, K_B2 = range(10)
A_I, A_A, A_A2, A_B, A_B2, A_R, A_R2 = range(7)


def kernel(img_hbm, txt_hbm, scale_ref, pair_ref, row_out, col_out,
           raw_i, raw_t, img, txt, relay, relay2, rm, rs, cm, cs, posr, posc, loc,
           stat_out, stat_in, ss, rsem, lsem, st_s, st_r):
    g = lax.axis_index("group")
    b = lax.axis_index("blk")
    j = b % 2
    x = (b // 2) % 4
    wrap3 = x // 3
    wrap2 = x // 2
    first1 = 1 - (x + 2) // 3
    first2 = 1 - x // 2

    def at(group, blk):
        return (group % 2, (blk + 2 * NBLK) % NBLK)

    row0 = b - 2 * x
    other_group = at(g + 1, b)
    other_core = at(g, b + 1 - 2 * j)
    nxt = at(g + j * wrap3, b + 2)
    nxt_from = at(g + j * first1, b - 2)
    xprev = at(g, row0 + 2 * ((x + 3) % 4))
    xprev_from = at(g, row0 + 2 * ((x + 1) % 4))
    row_next = at(g + j, b + 8)
    row_prev = at(g + j, b - 8)
    row_first = at(g, row0)
    row_last = at(g, row0 + 6)
    mate1 = at(g + (1 - j) * first1, b - 2 + 1 - 2 * j)
    mate1_from = at(g + j * wrap3, b + 2 + 1 - 2 * j)
    back2 = at(g + j * first2, b - 4)
    back2_from = at(g + j * wrap2, b + 4)
    mate2 = at(g + first2, b - 3)
    mate2_from = at(g + wrap2, b + 3)

    for q in range(NQ):
        sl = pl.ds(q * Q, Q)
        pltpu.make_async_copy(txt_hbm.at[sl], raw_t.at[sl], lsem.at[0, q]).start()
        pltpu.make_async_copy(img_hbm.at[sl], raw_i.at[sl], lsem.at[1, q]).start()

    barrier = pltpu.get_barrier_semaphore()

    def hello(dev):
        pl.semaphore_signal(barrier, inc=1, device_id=dev, device_id_type=MESH)

    hello(other_group)
    hello(other_core)
    hello(nxt_from)
    hello(xprev_from)
    hello(nxt)
    hello(mate1_from)
    hello(back2_from)

    @pl.when(x % 2 == 1)
    def _():
        hello(row_prev)

    @pl.when(x == 0)
    def _():
        hello(row_last)

    @pl.when(j == 1)
    def _():
        hello(mate2_from)

    rm[...] = jnp.full_like(rm, LOW)
    rs[...] = jnp.zeros_like(rs)
    cm[...] = jnp.full_like(cm, LOW)
    cs[...] = jnp.zeros_like(cs)
    posr[...] = jnp.zeros_like(posr)
    posc[...] = jnp.zeros_like(posc)
    base = (g * NBLK + b) * ROWS
    ids = (pair_ref[...] - base).astype(jnp.float32)
    loc[...] = jnp.transpose(jnp.broadcast_to(ids, (128, ROWS)))

    pl.semaphore_wait(barrier, 7 + x % 2 + wrap3 + 1 - j)

    def span(slot, q):
        return pl.ds(pl.multiple_of(slot * ROWS + q * Q, Q), Q)

    def push(kind, arrival, q, src, dst, dev):
        return pltpu.make_async_remote_copy(
            src_ref=src, dst_ref=dst, send_sem=ss.at[kind, q], recv_sem=rsem.at[arrival, q],
            device_id=dev, device_id_type=MESH)

    def arrived(arrival, q, dst):
        push(K_I, arrival, q, dst, dst, other_core).wait_recv()

    def c_i(q):
        return push(K_I, A_I, q, img.at[span(0, q)], img.at[span(1, q)], other_group)

    def c_a(q):
        return push(K_A, A_A, q, txt.at[span(0, q)], txt.at[span(1, q)], nxt)

    def c_c(q):
        return push(K_C, A_R, q, txt.at[span(0, q)], relay.at[span(0, q)], xprev)

    def c_t(q):
        return push(K_C, A_R2, q, txt.at[span(0, q)], relay2.at[span(0, q)], row_next)

    def c_o(q):
        return push(K_O, A_B2, q, txt.at[span(0, q)], txt.at[span(4, q)], other_core)

    def c_a2(q):
        return push(K_A2, A_A2, q, txt.at[span(1, q)], txt.at[span(2, q)], other_core)

    def c_b(q):
        return push(K_B, A_B, q, txt.at[span(1, q)], txt.at[span(3, q)], nxt)

    def c_r(q):
        return push(K_R, A_B, q, relay.at[span(0, q)], txt.at[span(3, q)], xprev)

    def c_r1(q):
        return push(K_R, A_R2, q, relay.at[span(0, q)], relay2.at[span(0, q)], row_next)

    def c_d(q):
        return push(K_R2, A_B, q, relay2.at[span(0, q)], txt.at[span(3, q)], xprev)

    def c_e(q):
        return push(K_R2, A_A, q, relay2.at[span(0, q)], txt.at[span(1, q)], row_first)

    def c_f(q):
        return push(K_R2B, A_R, q, relay2.at[span(0, q)], relay.at[span(0, q)], xprev)

    def c_b2(q):
        return push(K_B2, A_B2, q, txt.at[span(3, q)], txt.at[span(4, q)], other_core)

    def unit(raw):
        wide = raw.astype(jnp.float32)
        inverse = lax.rsqrt(jnp.mean(wide * wide, axis=-1, keepdims=True) + 1e-06)
        return (wide * inverse * D ** (-0.5)).astype(jnp.bfloat16)

    def own_piece(q, carry):
        sl = span(0, q)
        pltpu.make_async_copy(txt_hbm.at[sl], raw_t.at[sl], lsem.at[0, q]).wait()
        txt[sl, :] = unit(raw_t[sl, :])

        @pl.when((x < 3) | (q < NA))
        def _():
            c_a(q).start()

        @pl.when((x < 3) & (q >= NA))
        def _():
            c_c(q).start()

        @pl.when((x == 3) & (q >= NA))
        def _():
            c_t(q).start()

        @pl.when(j == 0)
        def _():
            c_o(q).start()

        pltpu.make_async_copy(img_hbm.at[sl], raw_i.at[sl], lsem.at[1, q]).wait()
        img[sl, :] = unit(raw_i[sl, :])
        c_i(q).start()
        return carry

    lax.fori_loop(0, NQ, own_piece, 0)

    sc = scale_ref[0] * LOG2E

    def scores(ip, tp):
        return lax.dot_general(
            img[pl.ds(pl.multiple_of(ip * MI, MI), MI), :], txt[pl.ds(pl.multiple_of(tp * NT, NT), NT), :],
            (((1,), (1,)), ((), ())), preferred_element_type=jnp.float32) * sc

    def tally(ip, tp, s):
        ri = pl.ds(pl.multiple_of(ip * MI, MI), MI)
        left, right = s[:, :128], s[:, 128:]
        ro = rm[ri, :]
        rn = jnp.maximum(ro, jnp.maximum(left, right))
        rs[ri, :] = rs[ri, :] * jnp.exp2(ro - rn) + (jnp.exp2(left - rn) + jnp.exp2(right - rn))
        rm[ri, :] = rn
        s3 = s.reshape(MI // 8, 8, NT)
        co = cm[tp]
        cn = jnp.maximum(co, jnp.max(s3, axis=0))
        cs[tp] = cs[tp] * jnp.exp2(co - cn) + jnp.sum(jnp.exp2(s3 - cn[None]), axis=0)
        cm[tp] = cn

    def own_tile(n, carry):
        ip, tp = n % 2, n // 2
        s = scores(ip, tp)
        ri = pl.ds(pl.multiple_of(ip * MI, MI), MI)
        lane = lax.broadcasted_iota(jnp.int32, (MI, 128), 1).astype(jnp.float32) + (tp * NT).astype(jnp.float32)
        want = loc[ri, :]
        left = jnp.where(want == lane, s[:, :128], 0.0)
        right = jnp.where(want == lane + 128.0, s[:, 128:], 0.0)
        posr[ri, :] = posr[ri, :] + left + right
        posc[tp, :, :128] = posc[tp, :, :128] + jnp.sum(left.reshape(MI // 8, 8, 128), axis=0)
        posc[tp, :, 128:] = posc[tp, :, 128:] + jnp.sum(right.reshape(MI // 8, 8, 128), axis=0)
        tally(ip, tp, s)
        return carry

    def sweep(i0, ni, t0, nt, stride):
        def one(n, carry):
            ip, tp = i0 + n % ni, t0 + (n // ni) * stride
            tally(ip, tp, scores(ip, tp))
            return carry
        lax.fori_loop(0, ni * nt, one, 0)

    def h_i(q):
        arrived(A_I, q, img.at[span(1, q)])

    def h_a(q):
        arrived(A_A, q, txt.at[span(1, q)])
        if q < NA:
            c_b(q).start()
        c_a2(q).start()

    def h_a2(q):
        arrived(A_A2, q, txt.at[span(2, q)])

    def h_b(q):
        arrived(A_B, q, txt.at[span(3, q)])

        @pl.when(j == 1)
        def _():
            c_b2(q).start()

    def h_b2(q):
        arrived(A_B2, q, txt.at[span(4, q)])

    def h_r(q):
        arrived(A_R, q, relay.at[span(0, q)])

        @pl.when(x == 1)
        def _():
            c_r1(q).start()

        @pl.when(x != 1)
        def _():
            c_r(q).start()

    def h_r2_last(q):
        @pl.when(x == 3)
        def _():
            arrived(A_R2, q, relay2.at[span(0, q)])
            c_e(q).start()
            c_f(q).start()

    def h_r2_second(q):
        @pl.when(x == 1)
        def _():
            arrived(A_R2, q, relay2.at[span(0, q)])
            c_d(q).start()

    lax.fori_loop(0, 6, own_tile, 0)
    h_r2_last(2); h_a(0); h_r(2)
    h_r2_last(3); h_a(1); h_r(3)
    h_a2(0); h_a2(1)
    sweep(0, 2, 3, 2, 3)
    h_r2_last(4); h_a(2); h_r(4); h_r2_second(2)
    h_r2_last(5); h_a(3); h_r(5); h_r2_second(3)
    h_a2(2); h_a2(3)
    sweep(0, 2, 4, 2, 3)
    h_i(0); h_i(1); h_i(2)
    sweep(2, 1, 0, 5, 1)
    sweep(2, 1, 6, 2, 1)
    h_r2_second(4); h_r2_second(5)
    h_a(4); h_a(5); h_a2(4); h_a2(5)
    sweep(0, 3, 5, 2, 3)
    h_b(2); h_b(3); h_b2(2); h_b2(3)
    sweep(0, 3, 10, 2, 3)
    h_i(3); h_i(4); h_i(5)
    sweep(3, 1, 0, 9, 1)
    sweep(3, 1, 10, 2, 3)
    h_b(0); h_b(1); h_b2(0); h_b2(1)
    sweep(0, 4, 9, 2, 3)
    h_b(4); h_b(5); h_b2(4); h_b2(5)
    sweep(0, 4, 11, 2, 3)

    def rows_of(part):
        ri = pl.ds(part * ROWS, ROWS)
        mt = jnp.transpose(rm[ri, :])
        st = jnp.transpose(rs[ri, :])
        top = jnp.max(mt, axis=0, keepdims=True)
        return top, jnp.sum(st * jnp.exp2(mt - top), axis=0, keepdims=True)

    def cols_of(slot, u):
        m = cm[slot * 3 + u]
        top = jnp.max(m, axis=0, keepdims=True)
        return top, jnp.sum(cs[slot * 3 + u] * jnp.exp2(m - top), axis=0, keepdims=True)

    def c_stat(k, to, dev):
        return pltpu.make_async_remote_copy(
            src_ref=stat_out.at[k], dst_ref=stat_in.at[to], send_sem=st_s.at[k], recv_sem=st_r.at[to],
            device_id=dev, device_id_type=MESH)

    top, total = rows_of(1)
    stat_out[0, 0:1, :] = top
    stat_out[0, 1:2, :] = total
    c_stat(0, 0, other_group).start()
    for slot in (1, 2, 3, 4):
        for u in range(3):
            top, total = cols_of(slot, u)
            stat_out[slot, 0:1, u * NT:(u + 1) * NT] = top
            stat_out[slot, 1:2, u * NT:(u + 1) * NT] = total
    def stat_sends(act):
        act(c_stat(1, 2, nxt_from))

        @pl.when(j == 0)
        def _():
            act(c_stat(2, 1, mate1))
            act(c_stat(4, 3, mate2))

        @pl.when(j == 1)
        def _():
            act(c_stat(2, 3, mate1))
            act(c_stat(4, 1, other_core))

        act(c_stat(3, 4, back2))

    stat_sends(lambda c: c.start())

    top, total = rows_of(0)
    positive = jnp.sum(jnp.transpose(posr[...]), axis=0, keepdims=True)
    for k in range(5):
        c_stat(0, k, other_core).wait_recv()
    mine = [cols_of(0, u) for u in range(3)]
    in_top, in_total = stat_in[0, 0:1, :], stat_in[0, 1:2, :]
    m = jnp.maximum(top, in_top)
    total = total * jnp.exp2(top - m) + in_total * jnp.exp2(in_top - m)
    row_out[...] = LN2 * (m - positive) + jnp.log(total)
    for u in range(3):
        ls = slice(u * NT, (u + 1) * NT)
        top, total = mine[u]
        m = top
        for k in range(1, 5):
            m = jnp.maximum(m, stat_in[k, 0:1, ls])
        total = total * jnp.exp2(top - m)
        for k in range(1, 5):
            total = total + stat_in[k, 1:2, ls] * jnp.exp2(stat_in[k, 0:1, ls] - m)
        pc = jnp.sum(posc[u], axis=0, keepdims=True)
        col_out[:, ls] = LN2 * (m - pc) + jnp.log(total)

    c_stat(0, 0, other_group).wait_send()
    stat_sends(lambda c: c.wait_send())

    def sent(q, carry):
        c_i(q).wait_send()
        c_a2(q).wait_send()

        @pl.when((x < 3) | (q < NA))
        def _():
            c_a(q).wait_send()

        @pl.when(q < NA)
        def _():
            c_b(q).wait_send()

        @pl.when(q >= NA)
        def _():
            c_c(q).wait_send()
            c_r(q).wait_send()

        @pl.when((q >= NA) & (x % 2 == 1))
        def _():
            c_d(q).wait_send()

        @pl.when((q >= NA) & (x == 3))
        def _():
            c_f(q).wait_send()

        @pl.when(j == 0)
        def _():
            c_o(q).wait_send()

        @pl.when(j == 1)
        def _():
            c_b2(q).wait_send()

        return carry

    lax.fori_loop(0, NQ, sent, 0)


def per_device(image_features, text_features, logit_scale, pair_ids):
    vmem = pl.BlockSpec(memory_space=pltpu.VMEM)
    anywhere = pl.BlockSpec(memory_space=pl.ANY)
    smem = pl.BlockSpec(memory_space=pltpu.SMEM)
    out = jax.ShapeDtypeStruct((1, ROWS), jnp.float32)
    row_gap, col_gap = pl.pallas_call(
        kernel,
        out_shape=(out, out),
        in_specs=[anywhere, anywhere, smem, vmem],
        out_specs=(vmem, vmem),
        scratch_shapes=[
            pltpu.VMEM((ROWS, D), jnp.bfloat16),
            pltpu.VMEM((ROWS, D), jnp.bfloat16),
            pltpu.VMEM((2 * ROWS, D), jnp.bfloat16),
            pltpu.VMEM((5 * ROWS, D), jnp.bfloat16),
            pltpu.VMEM((ROWS, D), jnp.bfloat16),
            pltpu.VMEM((ROWS, D), jnp.bfloat16),
            pltpu.VMEM((2 * ROWS, 128), jnp.float32),
            pltpu.VMEM((2 * ROWS, 128), jnp.float32),
            pltpu.VMEM((15, 8, NT), jnp.float32),
            pltpu.VMEM((15, 8, NT), jnp.float32),
            pltpu.VMEM((ROWS, 128), jnp.float32),
            pltpu.VMEM((3, 8, NT), jnp.float32),
            pltpu.VMEM((ROWS, 128), jnp.float32),
            pltpu.VMEM((5, 8, ROWS), jnp.float32),
            pltpu.VMEM((5, 8, ROWS), jnp.float32),
            pltpu.SemaphoreType.DMA((10, NQ)),
            pltpu.SemaphoreType.DMA((7, NQ)),
            pltpu.SemaphoreType.DMA((2, NQ)),
            pltpu.SemaphoreType.DMA((5,)),
            pltpu.SemaphoreType.DMA((5,)),
        ],
        compiler_params=pltpu.CompilerParams(
            collective_id=0, has_side_effects=True, vmem_limit_bytes=56 * 2**20),
        cost_estimate=pl.CostEstimate(flops=15 * 10**9, bytes_accessed=4 * 10**6, transcendentals=12 * 10**6),
    )(image_features, text_features, logit_scale, pair_ids.reshape(1, ROWS))
    return (row_gap.reshape(ROWS), col_gap.reshape(ROWS))


def solution(mesh):
    placed = (P(("group", "blk"), None), P(("group", "blk"), None), P(), P(("group", "blk")))
    return jax.shard_map(
        per_device,
        mesh=mesh,
        in_specs=placed,
        out_specs=(P(("group", "blk")), P(("group", "blk"))),
        check_vma=False,
    )
```

```python
import math

import jax
import jax.numpy as jnp
from jax import lax
from jax.experimental import pallas as pl
from jax.experimental.pallas import tpu as pltpu
from jax.sharding import PartitionSpec as P

MESH = pl.DeviceIdType.MESH
ROWS = 768
D = 1280
NBLK = 64
Q = 64
NQ = ROWS // Q
NA = 4
MI = 384
AHEAD = 2
SLOTS = 18
PACE = (3, 4)
HALF_AT, ALL_AT = 11, 17
T_AHEAD = 3
T_AT = 6
LAST_AT = 1
R0, R1, R2 = 0, 0, 3
R_EARLY, R3 = 5, 4
SECOND_AT = 4
B_AT = 6
C_B3 = 10
NT = 256
LOG2E = math.log2(math.e)
LN2 = math.log(2.0)
LOW = -1e30

K_I, K_A, K_C, K_O, K_A2, K_B, K_R, K_R2, K_R2B, K_B2 = range(10)
A_I, A_A, A_A2, A_B, A_B2, A_R, A_R2 = range(7)


OWN = [(5, 3), (6, 6), (9, 4), (10, 7), (13, 5), (13, 10), (14, 8), (14, 13)]
HALF = [(13, 20), (14, 26), (17, 21), (17, 27)]
WIDE = [(HALF_AT, 0), (13, 2), (14, 4), (17, 1), (17, 3), (17, 5)]
LAST = [(17, 9), (17, 11), (18, 12), (18, 14)]


def look(values, n):
    words = [sum(v << (6 * k) for k, v in enumerate(values[i:i + 5])) for i in range(0, len(values), 5)]
    word = words[0]
    for i in range(1, len(words)):
        word = jnp.where(n // 5 == i, words[i], word)
    return (word // (1 << (6 * (n % 5)))) % 64


def upto(tasks):
    return [sum(t[0] <= k for t in tasks) for k in range(SLOTS + 1)]


def kernel(img_hbm, txt_hbm, scale_ref, pair_ref, row_out, col_out,
           raw_i, raw_t, img, txt, relay, relay2, rm, rs, cm, cs, posr, posc, loc,
           stat_out, stat_in, ss, rsem, lsem, st_s, st_r):
    g = lax.axis_index("group")
    b = lax.axis_index("blk")
    j = b % 2
    x = (b // 2) % 4
    wrap3 = x // 3
    wrap2 = x // 2
    first1 = 1 - (x + 2) // 3
    first2 = 1 - x // 2

    def at(group, blk):
        return (group % 2, (blk + 2 * NBLK) % NBLK)

    row0 = b - 2 * x
    other_group = at(g + 1, b)
    other_core = at(g, b + 1 - 2 * j)
    nxt = at(g + j * wrap3, b + 2)
    nxt_from = at(g + j * first1, b - 2)
    xprev = at(g, row0 + 2 * ((x + 3) % 4))
    xprev_from = at(g, row0 + 2 * ((x + 1) % 4))
    row_next = at(g + j, b + 8)
    row_prev = at(g + j, b - 8)
    row_first = at(g, row0)
    row_last = at(g, row0 + 6)
    mate1 = at(g + (1 - j) * first1, b - 2 + 1 - 2 * j)
    mate1_from = at(g + j * wrap3, b + 2 + 1 - 2 * j)
    back2 = at(g + j * first2, b - 4)
    back2_from = at(g + j * wrap2, b + 4)
    mate2 = at(g + first2, b - 3)
    mate2_from = at(g + wrap2, b + 3)

    for q in range(NQ):
        sl = pl.ds(q * Q, Q)
        pltpu.make_async_copy(txt_hbm.at[sl], raw_t.at[sl], lsem.at[0, q]).start()
        pltpu.make_async_copy(img_hbm.at[sl], raw_i.at[sl], lsem.at[1, q]).start()

    barrier = pltpu.get_barrier_semaphore()

    def hello(dev):
        pl.semaphore_signal(barrier, inc=1, device_id=dev, device_id_type=MESH)

    hello(other_group)
    hello(other_core)
    hello(nxt_from)
    hello(xprev_from)
    hello(nxt)
    hello(mate1_from)
    hello(back2_from)

    @pl.when(x % 2 == 1)
    def _():
        hello(row_prev)

    @pl.when(x == 0)
    def _():
        hello(row_last)

    @pl.when(j == 1)
    def _():
        hello(mate2_from)

    rm[...] = jnp.full_like(rm, LOW)
    rs[...] = jnp.zeros_like(rs)
    cm[...] = jnp.full_like(cm, LOW)
    cs[...] = jnp.zeros_like(cs)
    posr[...] = jnp.zeros_like(posr)
    posc[...] = jnp.zeros_like(posc)
    base = (g * NBLK + b) * ROWS
    ids = (pair_ref[...] - base).astype(jnp.float32).reshape(1, ROWS)
    loc[...] = jnp.transpose(jnp.broadcast_to(ids, (128, ROWS)))

    pl.semaphore_wait(barrier, 7 + x % 2 + wrap3 + 1 - j)

    def span(slot, q):
        return pl.ds(pl.multiple_of(slot * ROWS + q * Q, Q), Q)

    def push(kind, arrival, q, src, dst, dev):
        return pltpu.make_async_remote_copy(
            src_ref=src, dst_ref=dst, send_sem=ss.at[kind, q], recv_sem=rsem.at[arrival, q],
            device_id=dev, device_id_type=MESH)

    def arrived(arrival, q, dst):
        push(K_I, arrival, q, dst, dst, other_core).wait_recv()

    def c_i(q):
        return push(K_I, A_I, q, img.at[span(0, q)], img.at[span(1, q)], other_group)

    def c_a(q):
        return push(K_A, A_A, q, txt.at[span(0, q)], txt.at[span(1, q)], nxt)

    def c_c(q):
        return push(K_C, A_R, q, txt.at[span(0, q)], relay.at[span(0, q)], xprev)

    def c_t(q):
        return push(K_C, A_R2, q, txt.at[span(0, q)], relay2.at[span(0, q)], row_next)

    def c_o(q):
        return push(K_O, A_B2, q, txt.at[span(0, q)], txt.at[span(4, q)], other_core)

    def c_a2(q):
        return push(K_A2, A_A2, q, txt.at[span(1, q)], txt.at[span(2, q)], other_core)

    def c_b(q):
        return push(K_B, A_B, q, txt.at[span(1, q)], txt.at[span(3, q)], nxt)

    def c_r(q):
        return push(K_R, A_B, q, relay.at[span(0, q)], txt.at[span(3, q)], xprev)

    def c_r1(q):
        return push(K_R, A_R2, q, relay.at[span(0, q)], relay2.at[span(0, q)], row_next)

    def c_d(q):
        return push(K_R2, A_B, q, relay2.at[span(0, q)], txt.at[span(3, q)], xprev)

    def c_e(q):
        return push(K_R2, A_A, q, relay2.at[span(0, q)], txt.at[span(1, q)], row_first)

    def c_f(q):
        return push(K_R2B, A_R, q, relay2.at[span(0, q)], relay.at[span(0, q)], xprev)

    def c_b2(q):
        return push(K_B2, A_B2, q, txt.at[span(3, q)], txt.at[span(4, q)], other_core)

    def unit(raw):
        wide = raw.astype(jnp.float32)
        inverse = lax.rsqrt(jnp.mean(wide * wide, axis=-1, keepdims=True) + 1e-06)
        return (wide * inverse * D ** (-0.5)).astype(jnp.bfloat16)

    def own_text(n, carry):
        q = n
        sl = span(0, q)
        pltpu.make_async_copy(txt_hbm.at[sl], raw_t.at[sl], lsem.at[0, q]).wait()
        txt[sl, :] = unit(raw_t[sl, :])

        @pl.when((x < 3) | (q < NA))
        def _():
            c_a(q).start()

        @pl.when((x < 3) & (q >= NA))
        def _():
            c_c(q).start()

        @pl.when((x == 3) & (q >= NA) & (q < NA + T_AHEAD))
        def _():
            c_t(q).start()

        @pl.when(j == 0)
        def _():
            c_o(q).start()

        return carry

    def own_image(q, carry):
        sl = span(0, q)
        pltpu.make_async_copy(img_hbm.at[sl], raw_i.at[sl], lsem.at[1, q]).wait()
        img[sl, :] = unit(raw_i[sl, :])

        @pl.when(q < AHEAD)
        def _():
            c_i(q).start()

        return carry

    lax.fori_loop(0, NQ, own_text, 0)
    lax.fori_loop(0, NQ, own_image, 0)

    sc = scale_ref[...].reshape(1, 1) * LOG2E

    def scores(ri, tp, n=1):
        return lax.dot_general(
            img[ri, :], txt[pl.ds(pl.multiple_of(tp * NT, NT), n * NT), :],
            (((1,), (1,)), ((), ())), preferred_element_type=jnp.float32) * sc

    def tally(ri, m, tp, s):
        n = s.shape[1] // 128
        parts = [s[:, k * 128:(k + 1) * 128] for k in range(n)]
        ro = rm[ri, :]
        rn = ro
        for part in parts:
            rn = jnp.maximum(rn, part)
        total = rs[ri, :] * jnp.exp2(ro - rn)
        for part in parts:
            total = total + jnp.exp2(part - rn)
        rs[ri, :] = total
        rm[ri, :] = rn
        for k in range(s.shape[1] // NT):
            s3 = s[:, k * NT:(k + 1) * NT].reshape(m // 8, 8, NT)
            co = cm[tp + k]
            cn = jnp.maximum(co, jnp.max(s3, axis=0))
            cs[tp + k] = cs[tp + k] * jnp.exp2(co - cn) + jnp.sum(jnp.exp2(s3 - cn[None]), axis=0)
            cm[tp + k] = cn

    whole = pl.ds(0, ROWS)

    def pair_tile(tp, carry):
        s = scores(whole, tp)
        lane = (lax.broadcasted_iota(jnp.int32, (ROWS, 128), 1) + tp * NT).astype(jnp.float32)
        want = loc[...]
        left = jnp.where(want == lane, s[:, :128], 0.0)
        right = jnp.where(want == lane + 128.0, s[:, 128:], 0.0)
        posr[...] = posr[...] + left + right
        posc[tp, :, :128] = jnp.sum(left.reshape(ROWS // 8, 8, 128), axis=0)
        posc[tp, :, 128:] = jnp.sum(right.reshape(ROWS // 8, 8, 128), axis=0)
        tally(whole, ROWS, tp, s)
        return carry

    def own_tile(n, carry):
        tp = look([t[1] for t in OWN], n)
        tally(whole, ROWS, tp, scores(whole, tp))
        return carry

    def half_tile(n, carry):
        code = look([t[1] for t in HALF], n)
        ri = pl.ds(pl.multiple_of(ROWS + (code % 2) * MI, MI), MI)
        tally(ri, MI, code // 2, scores(ri, code // 2))
        return carry

    def wide_tile(n, carry):
        code = look([t[1] for t in WIDE], n)
        ri = pl.ds(pl.multiple_of(ROWS + (code % 2) * MI, MI), MI)
        tp = (code // 2) * 3
        tally(ri, MI, tp, scores(ri, tp, 3))
        return carry

    def last_tile(n, carry):
        tp = look([t[1] for t in LAST], n)
        both = pl.ds(0, 2 * ROWS)
        tally(both, 2 * ROWS, tp, scores(both, tp))
        return carry

    lax.fori_loop(0, 3, pair_tile, 0)

    def within(q, lo, hi):
        return (q >= lo) & (q < hi)

    def slot(t, carry):
        q = t + T_AT

        @pl.when((x == 3) & within(q, NA + T_AHEAD, NQ))
        def _():
            c_t(q).start()

        q = t + LAST_AT

        @pl.when((x == 3) & within(q, NA, NQ))
        def _():
            arrived(A_R2, q, relay2.at[span(0, q)])
            c_e(q).start()
            c_f(q).start()

        early = within(t + 2, NA, NA + R_EARLY)
        q = jnp.where(x == 0, t - R0, jnp.where(x == 1, t - R1, jnp.where(x == 2, t - R2, jnp.where(early, t + 2, t - R3))))

        @pl.when(within(q, NA, NQ) & ((x < 3) | early | (q >= NA + R_EARLY)))
        def _():
            arrived(A_R, q, relay.at[span(0, q)])

            @pl.when(x == 1)
            def _():
                c_r1(q).start()

            @pl.when(x != 1)
            def _():
                c_r(q).start()

        q = t - 1 - first1

        @pl.when(within(q, 0, NQ))
        def _():
            arrived(A_A, q, txt.at[span(1, q)])

            @pl.when((q < NA) & (x < 3))
            def _():
                c_b(q).start()

            c_a2(q).start()

        @pl.when((x == 3) & within(t - C_B3, 0, NA))
        def _():
            c_b(t - C_B3).start()

        q = t - SECOND_AT

        @pl.when((x == 1) & within(q, NA, NQ))
        def _():
            arrived(A_R2, q, relay2.at[span(0, q)])
            c_d(q).start()

        def second(q):
            arrived(A_B, q, txt.at[span(3, q)])

            @pl.when(j == 1)
            def _():
                c_b2(q).start()

        @pl.when(within(t - B_AT, NA, NQ))
        def _():
            second(t - B_AT)

        @pl.when(within(t - 14, 0, NA))
        def _():
            second(t - 14)

        count = (t * PACE[0]) // PACE[1]
        q = count + AHEAD - 1

        @pl.when((count != ((t - 1) * PACE[0]) // PACE[1]) & within(q, AHEAD, NQ))
        def _():
            c_i(q).start()

        @pl.when((t == HALF_AT) | (t == ALL_AT))
        def _():
            def image(k, carry):
                arrived(A_I, k, img.at[span(1, k)])
                return carry
            half = (t // ALL_AT) * (NQ // 2)
            lax.fori_loop(half, half + NQ // 2, image, 0)

        @pl.when(within(t - 3, 0, NQ))
        def _():
            arrived(A_A2, t - 3, txt.at[span(2, t - 3)])

        @pl.when(within(t - 7, NA, NQ))
        def _():
            arrived(A_B2, t - 7, txt.at[span(4, t - 7)])

        @pl.when(within(t - 15, 0, NA))
        def _():
            arrived(A_B2, t - 15, txt.at[span(4, t - 15)])

        for tasks, tile in ((OWN, own_tile), (WIDE, wide_tile), (HALF, half_tile), (LAST, last_tile)):
            lax.fori_loop(look(upto(tasks), t - 1), look(upto(tasks), t), tile, 0)

        return carry

    lax.fori_loop(1, SLOTS + 1, slot, 0)

    def rows_of(part):
        ri = pl.ds(part * ROWS, ROWS)
        mt = jnp.transpose(rm[ri, :])
        st = jnp.transpose(rs[ri, :])
        top = jnp.max(mt, axis=0, keepdims=True)
        return top, jnp.sum(st * jnp.exp2(mt - top), axis=0, keepdims=True)

    def cols_of(slot, u):
        m = cm[slot * 3 + u]
        top = jnp.max(m, axis=0, keepdims=True)
        return top, jnp.sum(cs[slot * 3 + u] * jnp.exp2(m - top), axis=0, keepdims=True)

    def c_stat(k, to, dev):
        return pltpu.make_async_remote_copy(
            src_ref=stat_out.at[k], dst_ref=stat_in.at[to], send_sem=st_s.at[k], recv_sem=st_r.at[to],
            device_id=dev, device_id_type=MESH)

    top, total = rows_of(1)
    stat_out[0, 0:1, :] = top
    stat_out[0, 1:2, :] = total
    c_stat(0, 0, other_group).start()
    for slot in (1, 2, 3, 4):
        for u in range(3):
            top, total = cols_of(slot, u)
            stat_out[slot, 0:1, u * NT:(u + 1) * NT] = top
            stat_out[slot, 1:2, u * NT:(u + 1) * NT] = total
    def stat_sends(act):
        act(c_stat(1, 2, nxt_from))

        @pl.when(j == 0)
        def _():
            act(c_stat(2, 1, mate1))
            act(c_stat(4, 3, mate2))

        @pl.when(j == 1)
        def _():
            act(c_stat(2, 3, mate1))
            act(c_stat(4, 1, other_core))

        act(c_stat(3, 4, back2))

    stat_sends(lambda c: c.start())

    top, total = rows_of(0)
    positive = jnp.sum(jnp.transpose(posr[...]), axis=0, keepdims=True)
    for k in range(5):
        c_stat(0, k, other_core).wait_recv()
    mine = [cols_of(0, u) for u in range(3)]
    in_top, in_total = stat_in[0, 0:1, :], stat_in[0, 1:2, :]
    m = jnp.maximum(top, in_top)
    total = total * jnp.exp2(top - m) + in_total * jnp.exp2(in_top - m)
    row_out[...] = (LN2 * (m - positive) + jnp.log(total)).reshape(ROWS)
    for u in range(3):
        ls = slice(u * NT, (u + 1) * NT)
        top, total = mine[u]
        m = top
        for k in range(1, 5):
            m = jnp.maximum(m, stat_in[k, 0:1, ls])
        total = total * jnp.exp2(top - m)
        for k in range(1, 5):
            total = total + stat_in[k, 1:2, ls] * jnp.exp2(stat_in[k, 0:1, ls] - m)
        pc = jnp.sum(posc[u], axis=0, keepdims=True)
        col_out[ls] = (LN2 * (m - pc) + jnp.log(total)).reshape(NT)

    c_stat(0, 0, other_group).wait_send()
    stat_sends(lambda c: c.wait_send())

    def sent(q, carry):
        c_i(q).wait_send()
        c_a2(q).wait_send()

        @pl.when((x < 3) | (q < NA))
        def _():
            c_a(q).wait_send()

        @pl.when(q < NA)
        def _():
            c_b(q).wait_send()

        @pl.when(q >= NA)
        def _():
            c_c(q).wait_send()
            c_r(q).wait_send()

        @pl.when((q >= NA) & (x % 2 == 1))
        def _():
            c_d(q).wait_send()

        @pl.when((q >= NA) & (x == 3))
        def _():
            c_f(q).wait_send()

        @pl.when(j == 0)
        def _():
            c_o(q).wait_send()

        @pl.when(j == 1)
        def _():
            c_b2(q).wait_send()

        return carry

    lax.fori_loop(0, NQ, sent, 0)


def per_device(image_features, text_features, logit_scale, pair_ids):
    vmem = pl.BlockSpec(memory_space=pltpu.VMEM)
    anywhere = pl.BlockSpec(memory_space=pl.ANY)
    out = jax.ShapeDtypeStruct((ROWS,), jnp.float32)
    return pl.pallas_call(
        kernel,
        out_shape=(out, out),
        in_specs=[anywhere, anywhere, vmem, vmem],
        out_specs=(vmem, vmem),
        scratch_shapes=[
            pltpu.VMEM((ROWS, D), jnp.bfloat16),
            pltpu.VMEM((ROWS, D), jnp.bfloat16),
            pltpu.VMEM((2 * ROWS, D), jnp.bfloat16),
            pltpu.VMEM((5 * ROWS, D), jnp.bfloat16),
            pltpu.VMEM((ROWS, D), jnp.bfloat16),
            pltpu.VMEM((ROWS, D), jnp.bfloat16),
            pltpu.VMEM((2 * ROWS, 128), jnp.float32),
            pltpu.VMEM((2 * ROWS, 128), jnp.float32),
            pltpu.VMEM((15, 8, NT), jnp.float32),
            pltpu.VMEM((15, 8, NT), jnp.float32),
            pltpu.VMEM((ROWS, 128), jnp.float32),
            pltpu.VMEM((3, 8, NT), jnp.float32),
            pltpu.VMEM((ROWS, 128), jnp.float32),
            pltpu.VMEM((5, 8, ROWS), jnp.float32),
            pltpu.VMEM((5, 8, ROWS), jnp.float32),
            pltpu.SemaphoreType.DMA((10, NQ)),
            pltpu.SemaphoreType.DMA((7, NQ)),
            pltpu.SemaphoreType.DMA((2, NQ)),
            pltpu.SemaphoreType.DMA((5,)),
            pltpu.SemaphoreType.DMA((5,)),
        ],
        compiler_params=pltpu.CompilerParams(
            collective_id=0, has_side_effects=True, vmem_limit_bytes=56 * 2**20),
        cost_estimate=pl.CostEstimate(flops=15 * 10**9, bytes_accessed=4 * 10**6, transcendentals=12 * 10**6),
    )(image_features, text_features, logit_scale, pair_ids)


def solution(mesh):
    placed = (P(("group", "blk"), None), P(("group", "blk"), None), P(), P(("group", "blk")))
    return jax.shard_map(
        per_device,
        mesh=mesh,
        in_specs=placed,
        out_specs=(P(("group", "blk")), P(("group", "blk"))),
        check_vma=False,
    )
```

```python
import math

import jax
import jax.numpy as jnp
from jax import lax
from jax.experimental import pallas as pl
from jax.experimental.pallas import tpu as pltpu
from jax.sharding import PartitionSpec as P

MESH = pl.DeviceIdType.MESH
ROWS = 768
D = 1280
NBLK = 64
Q = 64
NQ = ROWS // Q
PART = 192
NA = 4
MI = 384
AHEAD = 2
SLOTS = 18
PACE = (3, 4)
HALF_AT, ALL_AT = 11, 17
T_AHEAD = 3
T_AT = 6
LAST_AT = 1
R0, R1, R2 = 0, 0, 3
R_EARLY, R3 = 5, 4
SECOND_AT = 4
B_AT = 6
C_B3 = 10
NT = 256
LOG2E = math.log2(math.e)
LN2 = math.log(2.0)
LOW = -1e30

K_I, K_A, K_C, K_O, K_A2, K_B, K_R, K_R2, K_R2B, K_B2 = range(10)
A_I, A_A, A_A2, A_B, A_B2, A_R, A_R2 = range(7)


OWN = [(5, 3), (6, 6), (9, 4), (10, 7), (13, 5), (13, 10), (14, 8), (14, 13)]
HALF = [(13, 20), (14, 26)]
WIDE = [(HALF_AT, 0), (13, 2), (14, 4), (17, 3), (17, 5)]
EARLY = [(15, 0), (16, 1)]
LAST = [(17, 0), (18, 1)]


def look(values, n):
    words = [sum(v << (6 * k) for k, v in enumerate(values[i:i + 5])) for i in range(0, len(values), 5)]
    word = words[0]
    for i in range(1, len(words)):
        word = jnp.where(n // 5 == i, words[i], word)
    return (word // (1 << (6 * (n % 5)))) % 64


def upto(tasks):
    return [sum(t[0] <= k for t in tasks) for k in range(SLOTS + 1)]


def kernel(img_hbm, txt_hbm, scale_hbm, pair_ref, gaps,
           raw_i, raw_t, img, txt, relay, relay2, rm, rs, cm, cs, posr, posc, loc, posv,
           stat_out, stat_in, ss, rsem, lsem, st_s, st_r, scale_ref, scale_sem):
    g = lax.axis_index("group")
    b = lax.axis_index("blk")
    j = b % 2
    x = (b // 2) % 4
    wrap3 = x // 3
    wrap2 = x // 2
    first1 = 1 - (x + 2) // 3
    first2 = 1 - x // 2

    def at(group, blk):
        return (group % 2, (blk + 2 * NBLK) % NBLK)

    row0 = b - 2 * x
    other_group = at(g + 1, b)
    other_core = at(g, b + 1 - 2 * j)
    nxt = at(g + j * wrap3, b + 2)
    nxt_from = at(g + j * first1, b - 2)
    xprev = at(g, row0 + 2 * ((x + 3) % 4))
    xprev_from = at(g, row0 + 2 * ((x + 1) % 4))
    row_next = at(g + j, b + 8)
    row_prev = at(g + j, b - 8)
    row_first = at(g, row0)
    row_last = at(g, row0 + 6)
    mate1 = at(g + (1 - j) * first1, b - 2 + 1 - 2 * j)
    mate1_from = at(g + j * wrap3, b + 2 + 1 - 2 * j)
    back2 = at(g + j * first2, b - 4)
    back2_from = at(g + j * wrap2, b + 4)
    mate2 = at(g + first2, b - 3)
    mate2_from = at(g + wrap2, b + 3)

    barrier = pltpu.get_barrier_semaphore()

    def hello(dev):
        pl.semaphore_signal(barrier, inc=1, device_id=dev, device_id_type=MESH)

    hello(nxt)
    hello(nxt_from)
    hello(mate1_from)
    hello(back2_from)

    @pl.when(j == 1)
    def _():
        hello(mate2_from)

    @pl.when(x % 2 == 1)
    def _():
        hello(row_prev)

    hello(other_group)
    hello(xprev_from)

    @pl.when(x == 0)
    def _():
        hello(row_last)

    hello(other_core)

    get_scale = pltpu.make_async_copy(scale_hbm, scale_ref, scale_sem)
    get_scale.start()

    def fetch(kind, n):
        sl = pl.ds(pl.multiple_of(n * PART, PART), PART)
        src, dst = ((txt_hbm, raw_t), (img_hbm, raw_i))[kind]
        return pltpu.make_async_copy(src.at[sl], dst.at[sl], lsem.at[kind, n])

    for kind in range(2):
        for n in range(ROWS // PART):
            fetch(kind, n).start()

    rm[...] = jnp.full_like(rm, LOW)
    rs[...] = jnp.zeros_like(rs)
    cm[...] = jnp.full_like(cm, LOW)
    cs[...] = jnp.zeros_like(cs)
    posr[...] = jnp.zeros_like(posr)
    posc[...] = jnp.zeros_like(posc)
    base = (g * NBLK + b) * ROWS
    ids = (pair_ref[...] - base).astype(jnp.float32).reshape(1, ROWS)
    loc[...] = jnp.transpose(jnp.broadcast_to(ids, (128, ROWS)))

    pl.semaphore_wait(barrier, 7 + x % 2 + wrap3 + 1 - j)

    def span(slot, q):
        return pl.ds(pl.multiple_of(slot * ROWS + q * Q, Q), Q)

    def push(kind, arrival, q, src, dst, dev):
        return pltpu.make_async_remote_copy(
            src_ref=src, dst_ref=dst, send_sem=ss.at[kind, q], recv_sem=rsem.at[arrival, q],
            device_id=dev, device_id_type=MESH)

    def arrived(arrival, q, dst):
        push(K_I, arrival, q, dst, dst, other_core).wait_recv()

    def c_i(q):
        return push(K_I, A_I, q, img.at[span(0, q)], img.at[span(1, q)], other_group)

    def c_a(q):
        return push(K_A, A_A, q, txt.at[span(0, q)], txt.at[span(1, q)], nxt)

    def c_c(q):
        return push(K_C, A_R, q, txt.at[span(0, q)], relay.at[span(0, q)], xprev)

    def c_t(q):
        return push(K_C, A_R2, q, txt.at[span(0, q)], relay2.at[span(0, q)], row_next)

    def c_o(q):
        return push(K_O, A_B2, q, txt.at[span(0, q)], txt.at[span(4, q)], other_core)

    def c_a2(q):
        return push(K_A2, A_A2, q, txt.at[span(1, q)], txt.at[span(2, q)], other_core)

    def c_b(q):
        return push(K_B, A_B, q, txt.at[span(1, q)], txt.at[span(3, q)], nxt)

    def c_r(q):
        return push(K_R, A_B, q, relay.at[span(0, q)], txt.at[span(3, q)], xprev)

    def c_r1(q):
        return push(K_R, A_R2, q, relay.at[span(0, q)], relay2.at[span(0, q)], row_next)

    def c_d(q):
        return push(K_R2, A_B, q, relay2.at[span(0, q)], txt.at[span(3, q)], xprev)

    def c_e(q):
        return push(K_R2, A_A, q, relay2.at[span(0, q)], txt.at[span(1, q)], row_first)

    def c_f(q):
        return push(K_R2B, A_R, q, relay2.at[span(0, q)], relay.at[span(0, q)], xprev)

    def c_b2(q):
        return push(K_B2, A_B2, q, txt.at[span(3, q)], txt.at[span(4, q)], other_core)

    def unit(raw):
        wide = raw.astype(jnp.float32)
        inverse = lax.rsqrt(jnp.mean(wide * wide, axis=-1, keepdims=True) + 1e-06)
        return (wide * inverse * D ** (-0.5)).astype(jnp.bfloat16)

    def own_text(n, carry):
        q = n
        sl = span(0, q)
        @pl.when(q % (PART // Q) == 0)
        def _():
            fetch(0, q // (PART // Q)).wait()

        txt[sl, :] = unit(raw_t[sl, :])

        @pl.when((x < 3) | (q < NA))
        def _():
            c_a(q).start()

        @pl.when((x < 3) & (q >= NA))
        def _():
            c_c(q).start()

        @pl.when((x == 3) & (q >= NA) & (q < NA + T_AHEAD))
        def _():
            c_t(q).start()

        @pl.when(j == 0)
        def _():
            c_o(q).start()

        return carry

    def own_image(q, carry):
        sl = span(0, q)

        @pl.when(q % (PART // Q) == 0)
        def _():
            fetch(1, q // (PART // Q)).wait()

        img[sl, :] = unit(raw_i[sl, :])

        @pl.when(q < AHEAD)
        def _():
            c_i(q).start()

        return carry

    lax.fori_loop(0, NQ, own_text, 0)
    lax.fori_loop(0, NQ, own_image, 0)

    get_scale.wait()
    sc = scale_ref[0] * LOG2E

    def mixed_text(tp, odd):
        at0 = pl.multiple_of(tp * NT + odd * 128, 128)
        return jnp.concatenate([txt[pl.ds(at0, 128), :], txt[pl.ds(at0 + 2 * NT, 128), :]], axis=0)

    def text_of(tp):
        return txt[pl.ds(pl.multiple_of(tp * NT, NT), NT), :]

    def scores(ri, text):
        return lax.dot_general(
            img[ri, :], text, (((1,), (1,)), ((), ())), preferred_element_type=jnp.float32) * sc

    def tally(ri, m, cols, s):
        n = s.shape[1] // 128
        parts = [s[:, k * 128:(k + 1) * 128] for k in range(n)]
        ro = rm[ri, :]
        rn = ro
        for part in parts:
            rn = jnp.maximum(rn, part)
        total = rs[ri, :] * jnp.exp2(ro - rn)
        for part in parts:
            total = total + jnp.exp2(part - rn)
        rs[ri, :] = total
        rm[ri, :] = rn
        for k in range(n):
            c = cols(k)
            s3 = parts[k].reshape(m // 8, 8, 128)
            co = cm[c]
            cn = jnp.maximum(co, jnp.max(s3, axis=0))
            cs[c] = cs[c] * jnp.exp2(co - cn) + jnp.sum(jnp.exp2(s3 - cn[None]), axis=0)
            cm[c] = cn

    whole = pl.ds(0, ROWS)

    def pair_tile(tp, carry):
        s = scores(whole, text_of(tp))
        lane = (lax.broadcasted_iota(jnp.int32, (ROWS, 128), 1) + tp * NT).astype(jnp.float32)
        want = loc[...]
        left = jnp.where(want == lane, s[:, :128], 0.0)
        right = jnp.where(want == lane + 128.0, s[:, 128:], 0.0)
        posr[...] = posr[...] + (left + right)
        posc[tp, :, :128] = jnp.sum(left.reshape(ROWS // 8, 8, 128), axis=0)
        posc[tp, :, 128:] = jnp.sum(right.reshape(ROWS // 8, 8, 128), axis=0)
        tally(whole, ROWS, lambda k: 2 * tp + k, s)
        return carry

    def own_tile(n, carry):
        tp = look([t[1] for t in OWN], n)
        tally(whole, ROWS, lambda k: 2 * tp + k, scores(whole, text_of(tp)))
        return carry

    def chain(*items):
        ahead = scores(items[0][0], items[0][3]())
        for k, (ri, m, cols, _) in enumerate(items):
            here = ahead
            if k + 1 < len(items):
                ahead = scores(items[k + 1][0], items[k + 1][3]())
            tally(ri, m, cols, here)

    def panel(ri, m, tp):
        return (ri, m, lambda k: 2 * tp + k, lambda: text_of(tp))

    def mixed(ri, m, slot, odd):
        return (ri, m, lambda k: 6 * slot + odd + 4 * k, lambda: mixed_text(3 * slot, odd))

    def half_rows(code):
        return pl.ds(pl.multiple_of(ROWS + (code % 2) * MI, MI), MI)

    def half_tile(n, carry):
        code = look([t[1] for t in HALF], n)
        chain(panel(half_rows(code), MI, code // 2))
        return carry

    def wide(code):
        chain(*[panel(half_rows(code), MI, (code // 2) * 3 + u) for u in range(3)])

    def wide_tile(n, carry):
        wide(look([t[1] for t in WIDE], n))
        return carry

    most, other, final = pl.ds(0, ROWS + MI), pl.ds(ROWS, ROWS), pl.ds(ROWS + MI, MI)

    def early_tile(n, carry):
        chain(mixed(most, ROWS + MI, 3 + n, 0))
        return carry

    def last_tile(n, carry):
        chain(panel(final, MI, 10 + 3 * n), mixed(final, MI, 3 + n, 0),
              mixed(whole, ROWS, 3 + n, 1), mixed(other, ROWS, 3 + n, 1))
        return carry

    lax.fori_loop(0, 3, pair_tile, 0)
    posv[...] = jnp.sum(jnp.transpose(posr[...]), axis=0, keepdims=True)

    def within(q, lo, hi):
        return (q >= lo) & (q < hi)

    def slot(t, carry):
        q = t + T_AT

        @pl.when((x == 3) & within(q, NA + T_AHEAD, NQ))
        def _():
            c_t(q).start()

        q = t + LAST_AT

        @pl.when((x == 3) & within(q, NA, NQ))
        def _():
            arrived(A_R2, q, relay2.at[span(0, q)])
            c_e(q).start()
            c_f(q).start()

        early = within(t + 2, NA, NA + R_EARLY)
        q = jnp.where(x == 0, t - R0, jnp.where(x == 1, t - R1, jnp.where(x == 2, t - R2, jnp.where(early, t + 2, t - R3))))

        @pl.when(within(q, NA, NQ) & ((x < 3) | early | (q >= NA + R_EARLY)))
        def _():
            arrived(A_R, q, relay.at[span(0, q)])

            @pl.when(x == 1)
            def _():
                c_r1(q).start()

            @pl.when(x != 1)
            def _():
                c_r(q).start()

        q = t - 1 - first1

        @pl.when(within(q, 0, NQ))
        def _():
            arrived(A_A, q, txt.at[span(1, q)])

            @pl.when((q < NA) & (x < 3))
            def _():
                c_b(q).start()

            c_a2(q).start()

        @pl.when((x == 3) & within(t - C_B3, 0, NA))
        def _():
            c_b(t - C_B3).start()

        q = t - SECOND_AT

        @pl.when((x == 1) & within(q, NA, NQ))
        def _():
            arrived(A_R2, q, relay2.at[span(0, q)])
            c_d(q).start()

        def second(q):
            arrived(A_B, q, txt.at[span(3, q)])

            @pl.when(j == 1)
            def _():
                c_b2(q).start()

        @pl.when(within(t - B_AT, NA, NQ))
        def _():
            second(t - B_AT)

        @pl.when(within(t - 14, 0, NA))
        def _():
            second(t - 14)

        count = (t * PACE[0]) // PACE[1]
        q = count + AHEAD - 1

        @pl.when((count != ((t - 1) * PACE[0]) // PACE[1]) & within(q, AHEAD, NQ))
        def _():
            c_i(q).start()

        @pl.when((t == HALF_AT) | (t == ALL_AT))
        def _():
            def image(k, carry):
                arrived(A_I, k, img.at[span(1, k)])
                return carry
            half = (t // ALL_AT) * (NQ // 2)
            lax.fori_loop(half, half + NQ // 2, image, 0)

        @pl.when(within(t - 3, 0, NQ))
        def _():
            arrived(A_A2, t - 3, txt.at[span(2, t - 3)])

        @pl.when(within(t - 7, NA, NQ))
        def _():
            arrived(A_B2, t - 7, txt.at[span(4, t - 7)])

        @pl.when(within(t - 15, 0, NA))
        def _():
            arrived(A_B2, t - 15, txt.at[span(4, t - 15)])

        for tasks, tile in (
            (OWN, own_tile), (WIDE, wide_tile), (HALF, half_tile), (EARLY, early_tile), (LAST, last_tile),
        ):
            lax.fori_loop(look(upto(tasks), t - 1), look(upto(tasks), t), tile, 0)

        return carry

    lax.fori_loop(1, SLOTS + 1, slot, 0)

    def rows_of(part):
        ri = pl.ds(part * ROWS, ROWS)
        mt = jnp.transpose(rm[ri, :])
        st = jnp.transpose(rs[ri, :])
        top = jnp.max(mt, axis=0, keepdims=True)
        return top, jnp.sum(st * jnp.exp2(mt - top), axis=0, keepdims=True)

    def cols_of(slot, u):
        m = cm[slot * 6 + u]
        top = jnp.max(m, axis=0, keepdims=True)
        return top, jnp.sum(cs[slot * 6 + u] * jnp.exp2(m - top), axis=0, keepdims=True)

    def c_stat(k, to, dev):
        return pltpu.make_async_remote_copy(
            src_ref=stat_out.at[k], dst_ref=stat_in.at[to], send_sem=st_s.at[k], recv_sem=st_r.at[to],
            device_id=dev, device_id_type=MESH)

    for slot in (1, 2, 3, 4):
        for u in range(6):
            top, total = cols_of(slot, u)
            stat_out[slot, 0:1, u * 128:(u + 1) * 128] = top
            stat_out[slot, 1:2, u * 128:(u + 1) * 128] = total

    def stat_sends(act):
        act(c_stat(1, 2, nxt_from))

        @pl.when(j == 0)
        def _():
            act(c_stat(2, 1, mate1))
            act(c_stat(4, 3, mate2))

        @pl.when(j == 1)
        def _():
            act(c_stat(2, 3, mate1))
            act(c_stat(4, 1, other_core))

        act(c_stat(3, 4, back2))

    stat_sends(lambda c: c.start())
    wide(1)
    top, total = rows_of(1)
    stat_out[0, 0:1, :] = top
    stat_out[0, 1:2, :] = total
    c_stat(0, 0, other_group).start()

    own_top, own_total = rows_of(0)
    mine = [cols_of(0, u) for u in range(6)]
    positive = posv[...]
    def sent(q, carry):
        c_i(q).wait_send()
        c_a2(q).wait_send()

        @pl.when((x < 3) | (q < NA))
        def _():
            c_a(q).wait_send()

        @pl.when(q < NA)
        def _():
            c_b(q).wait_send()

        @pl.when(q >= NA)
        def _():
            c_c(q).wait_send()
            c_r(q).wait_send()

        @pl.when((q >= NA) & (x % 2 == 1))
        def _():
            c_d(q).wait_send()

        @pl.when((q >= NA) & (x == 3))
        def _():
            c_f(q).wait_send()

        @pl.when(j == 0)
        def _():
            c_o(q).wait_send()

        @pl.when(j == 1)
        def _():
            c_b2(q).wait_send()

        return carry

    lax.fori_loop(0, NQ, sent, 0)

    for k in range(5):
        c_stat(0, k, other_core).wait_recv()
    in_top, in_total = stat_in[0, 0:1, :], stat_in[0, 1:2, :]
    m = jnp.maximum(own_top, in_top)
    total = own_total * jnp.exp2(own_top - m) + in_total * jnp.exp2(in_top - m)
    gaps[:ROWS] = (LN2 * (m - positive) + jnp.log(total)).reshape(ROWS)
    for u in range(6):
        ls = slice(u * 128, (u + 1) * 128)
        top, total = mine[u]
        m = top
        for k in range(1, 5):
            m = jnp.maximum(m, stat_in[k, 0:1, ls])
        total = total * jnp.exp2(top - m)
        for k in range(1, 5):
            total = total + stat_in[k, 1:2, ls] * jnp.exp2(stat_in[k, 0:1, ls] - m)
        pc = jnp.sum(posc[u // 2, :, u % 2 * 128:(u % 2 + 1) * 128], axis=0, keepdims=True)
        gaps[ROWS + u * 128:ROWS + (u + 1) * 128] = (LN2 * (m - pc) + jnp.log(total)).reshape(128)

    c_stat(0, 0, other_group).wait_send()
    stat_sends(lambda c: c.wait_send())


def per_device(image_features, text_features, logit_scale, pair_ids):
    vmem = pl.BlockSpec(memory_space=pltpu.VMEM)
    anywhere = pl.BlockSpec(memory_space=pl.ANY)
    out = jax.ShapeDtypeStruct((2 * ROWS,), jnp.float32)
    both = pl.pallas_call(
        kernel,
        out_shape=out,
        in_specs=[anywhere, anywhere, pl.BlockSpec(memory_space=pltpu.HBM), vmem],
        out_specs=vmem,
        scratch_shapes=[
            pltpu.VMEM((ROWS, D), jnp.bfloat16),
            pltpu.VMEM((ROWS, D), jnp.bfloat16),
            pltpu.VMEM((2 * ROWS, D), jnp.bfloat16),
            pltpu.VMEM((5 * ROWS, D), jnp.bfloat16),
            pltpu.VMEM((ROWS, D), jnp.bfloat16),
            pltpu.VMEM((ROWS, D), jnp.bfloat16),
            pltpu.VMEM((2 * ROWS, 128), jnp.float32),
            pltpu.VMEM((2 * ROWS, 128), jnp.float32),
            pltpu.VMEM((30, 8, 128), jnp.float32),
            pltpu.VMEM((30, 8, 128), jnp.float32),
            pltpu.VMEM((ROWS, 128), jnp.float32),
            pltpu.VMEM((3, 8, NT), jnp.float32),
            pltpu.VMEM((ROWS, 128), jnp.float32),
            pltpu.VMEM((1, ROWS), jnp.float32),
            pltpu.VMEM((5, 8, ROWS), jnp.float32),
            pltpu.VMEM((5, 8, ROWS), jnp.float32),
            pltpu.SemaphoreType.DMA((10, NQ)),
            pltpu.SemaphoreType.DMA((7, NQ)),
            pltpu.SemaphoreType.DMA((2, ROWS // PART)),
            pltpu.SemaphoreType.DMA((5,)),
            pltpu.SemaphoreType.DMA((5,)),
            pltpu.SMEM((1,), jnp.float32),
            pltpu.SemaphoreType.DMA,
        ],
        compiler_params=pltpu.CompilerParams(
            collective_id=0, has_side_effects=True, vmem_limit_bytes=56 * 2**20),
        cost_estimate=pl.CostEstimate(flops=15 * 10**9, bytes_accessed=4 * 10**6, transcendentals=12 * 10**6),
    )(image_features, text_features, logit_scale, pair_ids)
    return both[:ROWS], both[ROWS:]


def solution(mesh):
    placed = (P(("group", "blk"), None), P(("group", "blk"), None), P(), P(("group", "blk")))
    return jax.shard_map(
        per_device,
        mesh=mesh,
        in_specs=placed,
        out_specs=(P(("group", "blk")), P(("group", "blk"))),
        check_vma=False,
    )
```

```python
import math

import jax
import jax.numpy as jnp
from jax import lax
from jax.experimental import pallas as pl
from jax.experimental.pallas import tpu as pltpu
from jax.sharding import PartitionSpec as P

MESH = pl.DeviceIdType.MESH
ROWS = 768
D = 1280
NBLK = 64
Q = 64
NQ = ROWS // Q
PART = 192
NA = 4
MI = 384
AHEAD = 2
SLOTS = 18
PACE = (3, 4)
HALF_AT, ALL_AT = 11, 17
T_AHEAD = 5
T_AT = 8
LAST_AT = 1
R0, R1, R2 = 0, 0, 3
R_EARLY, R3 = 5, 4
SECOND_AT = 4
B_AT = 6
C_B3 = 10
NT = 256
LOG2E = math.log2(math.e)
LN2 = math.log(2.0)
LOW = -1e30

K_I, K_A, K_C, K_O, K_A2, K_B, K_R, K_R2, K_R2B, K_B2 = range(10)
A_I, A_A, A_A2, A_B, A_B2, A_R, A_R2 = range(7)


OWN = [(5, 3), (6, 6), (9, 4), (10, 7), (13, 5), (13, 10), (14, 8), (14, 13)]
HALF = [(13, 20), (14, 26)]
WIDE = [(HALF_AT, 0), (13, 2), (14, 4)]
EARLY = [(15, 0), (16, 1)]
LAST = [(17, 0), (18, 1)]


def look(values, n):
    words = [sum(v << (6 * k) for k, v in enumerate(values[i:i + 5])) for i in range(0, len(values), 5)]
    word = words[0]
    for i in range(1, len(words)):
        word = jnp.where(n // 5 == i, words[i], word)
    return (word // (1 << (6 * (n % 5)))) % 64


def upto(tasks):
    return [sum(t[0] <= k for t in tasks) for k in range(SLOTS + 1)]


def kernel(img_hbm, txt_hbm, scale_hbm, pair_ref, gaps,
           raw_i, raw_t, img, txt, relay, relay2, rm, rs, cm, cs, posr, posc, loc, posv,
           stat_out, stat_in, ss, rsem, lsem, st_s, st_r, scale_ref, scale_sem):
    g = lax.axis_index("group")
    b = lax.axis_index("blk")
    j = b % 2
    x = (b // 2) % 4
    wrap3 = x // 3
    wrap2 = x // 2
    first1 = 1 - (x + 2) // 3
    first2 = 1 - x // 2

    def at(group, blk):
        return (group % 2, (blk + 2 * NBLK) % NBLK)

    row0 = b - 2 * x
    other_group = at(g + 1, b)
    other_core = at(g, b + 1 - 2 * j)
    nxt = at(g + j * wrap3, b + 2)
    nxt_from = at(g + j * first1, b - 2)
    xprev = at(g, row0 + 2 * ((x + 3) % 4))
    xprev_from = at(g, row0 + 2 * ((x + 1) % 4))
    row_next = at(g + j, b + 8)
    row_prev = at(g + j, b - 8)
    row_first = at(g, row0)
    row_last = at(g, row0 + 6)
    mate1 = at(g + (1 - j) * first1, b - 2 + 1 - 2 * j)
    mate1_from = at(g + j * wrap3, b + 2 + 1 - 2 * j)
    back2 = at(g + j * first2, b - 4)
    back2_from = at(g + j * wrap2, b + 4)
    mate2 = at(g + first2, b - 3)
    mate2_from = at(g + wrap2, b + 3)

    def fetch(kind, n):
        sl = pl.ds(pl.multiple_of(n * PART, PART), PART)
        src, dst = ((txt_hbm, raw_t), (img_hbm, raw_i))[kind]
        return pltpu.make_async_copy(src.at[sl], dst.at[sl], lsem.at[kind, n])

    fetch(0, 0).start()

    barrier = pltpu.get_barrier_semaphore()

    def hello(dev):
        pl.semaphore_signal(barrier, inc=1, device_id=dev, device_id_type=MESH)

    hello(nxt)
    hello(nxt_from)
    hello(mate1_from)
    hello(back2_from)

    @pl.when(j == 1)
    def _():
        hello(mate2_from)

    @pl.when(x % 2 == 1)
    def _():
        hello(row_prev)

    hello(other_group)
    hello(xprev_from)

    @pl.when(x == 0)
    def _():
        hello(row_last)

    hello(other_core)

    get_scale = pltpu.make_async_copy(scale_hbm, scale_ref, scale_sem)
    get_scale.start()

    for kind in range(2):
        for n in range(1 - kind, ROWS // PART):
            fetch(kind, n).start()

    pl.semaphore_wait(barrier, 7 + x % 2 + wrap3 + 1 - j)

    def span(slot, q):
        return pl.ds(pl.multiple_of(slot * ROWS + q * Q, Q), Q)

    def push(kind, arrival, q, src, dst, dev):
        return pltpu.make_async_remote_copy(
            src_ref=src, dst_ref=dst, send_sem=ss.at[kind, q], recv_sem=rsem.at[arrival, q],
            device_id=dev, device_id_type=MESH)

    def arrived(arrival, q, dst):
        push(K_I, arrival, q, dst, dst, other_core).wait_recv()

    def c_i(q):
        return push(K_I, A_I, q, img.at[span(0, q)], img.at[span(1, q)], other_group)

    def c_a(q):
        return push(K_A, A_A, q, txt.at[span(0, q)], txt.at[span(1, q)], nxt)

    def c_c(q):
        return push(K_C, A_R, q, txt.at[span(0, q)], relay.at[span(0, q)], xprev)

    def c_t(q):
        return push(K_C, A_R2, q, txt.at[span(0, q)], relay2.at[span(0, q)], row_next)

    def c_o(q):
        return push(K_O, A_B2, q, txt.at[span(0, q)], txt.at[span(4, q)], other_core)

    def c_a2(q):
        return push(K_A2, A_A2, q, txt.at[span(1, q)], txt.at[span(2, q)], other_core)

    def c_b(q):
        return push(K_B, A_B, q, txt.at[span(1, q)], txt.at[span(3, q)], nxt)

    def c_r(q):
        return push(K_R, A_B, q, relay.at[span(0, q)], txt.at[span(3, q)], xprev)

    def c_r1(q):
        return push(K_R, A_R2, q, relay.at[span(0, q)], relay2.at[span(0, q)], row_next)

    def c_d(q):
        return push(K_R2, A_B, q, relay2.at[span(0, q)], txt.at[span(3, q)], xprev)

    def c_e(q):
        return push(K_R2, A_A, q, relay2.at[span(0, q)], txt.at[span(1, q)], row_first)

    def c_f(q):
        return push(K_R2B, A_R, q, relay2.at[span(0, q)], relay.at[span(0, q)], xprev)

    def c_b2(q):
        return push(K_B2, A_B2, q, txt.at[span(3, q)], txt.at[span(4, q)], other_core)

    def unit(raw):
        wide = raw.astype(jnp.float32)
        inverse = lax.rsqrt(jnp.mean(wide * wide, axis=-1, keepdims=True) + 1e-06)
        return (wide * inverse * D ** (-0.5)).astype(jnp.bfloat16)

    def own_text(n, carry):
        q = n
        sl = span(0, q)
        @pl.when(q % (PART // Q) == 0)
        def _():
            fetch(0, q // (PART // Q)).wait()

        txt[sl, :] = unit(raw_t[sl, :])

        @pl.when((x < 3) | (q < NA))
        def _():
            c_a(q).start()

        @pl.when((x < 3) & (q >= NA))
        def _():
            c_c(q).start()

        @pl.when((x == 3) & (q >= NA) & (q < NA + T_AHEAD))
        def _():
            c_t(q).start()

        @pl.when(j == 0)
        def _():
            c_o(q).start()

        return carry

    def own_image(q, carry):
        sl = span(0, q)

        @pl.when(q % (PART // Q) == 0)
        def _():
            fetch(1, q // (PART // Q)).wait()

        img[sl, :] = unit(raw_i[sl, :])

        @pl.when(q < AHEAD)
        def _():
            c_i(q).start()

        return carry

    lax.fori_loop(0, NQ, own_text, 0)
    lax.fori_loop(0, NQ, own_image, 0)

    rm[...] = jnp.full_like(rm, LOW)
    rs[...] = jnp.zeros_like(rs)
    cm[...] = jnp.full_like(cm, LOW)
    cs[...] = jnp.zeros_like(cs)
    posr[...] = jnp.zeros_like(posr)
    posc[...] = jnp.zeros_like(posc)
    base = (g * NBLK + b) * ROWS
    ids = (pair_ref[...] - base).astype(jnp.float32).reshape(1, ROWS)
    loc[...] = jnp.transpose(jnp.broadcast_to(ids, (128, ROWS)))

    get_scale.wait()
    sc = scale_ref[0] * LOG2E

    def mixed_text(tp, odd):
        at0 = pl.multiple_of(tp * NT + odd * 128, 128)
        return jnp.concatenate([txt[pl.ds(at0, 128), :], txt[pl.ds(at0 + 2 * NT, 128), :]], axis=0)

    def text_of(tp):
        return txt[pl.ds(pl.multiple_of(tp * NT, NT), NT), :]

    def scores(ri, text):
        return lax.dot_general(
            img[ri, :], text, (((1,), (1,)), ((), ())), preferred_element_type=jnp.float32) * sc

    def tally(ri, m, cols, s):
        n = s.shape[1] // 128
        parts = [s[:, k * 128:(k + 1) * 128] for k in range(n)]
        ro = rm[ri, :]
        rn = ro
        for part in parts:
            rn = jnp.maximum(rn, part)
        total = rs[ri, :] * jnp.exp2(ro - rn)
        for part in parts:
            total = total + jnp.exp2(part - rn)
        rs[ri, :] = total
        rm[ri, :] = rn
        for k in range(n):
            c = cols(k)
            s3 = parts[k].reshape(m // 8, 8, 128)
            co = cm[c]
            cn = jnp.maximum(co, jnp.max(s3, axis=0))
            cs[c] = cs[c] * jnp.exp2(co - cn) + jnp.sum(jnp.exp2(s3 - cn[None]), axis=0)
            cm[c] = cn

    whole = pl.ds(0, ROWS)

    def pair_tile(tp, carry):
        s = scores(whole, text_of(tp))
        lane = (lax.broadcasted_iota(jnp.int32, (ROWS, 128), 1) + tp * NT).astype(jnp.float32)
        want = loc[...]
        left = jnp.where(want == lane, s[:, :128], 0.0)
        right = jnp.where(want == lane + 128.0, s[:, 128:], 0.0)
        posr[...] = posr[...] + (left + right)
        posc[tp, :, :128] = jnp.sum(left.reshape(ROWS // 8, 8, 128), axis=0)
        posc[tp, :, 128:] = jnp.sum(right.reshape(ROWS // 8, 8, 128), axis=0)
        tally(whole, ROWS, lambda k: 2 * tp + k, s)
        return carry

    def own_tile(n, carry):
        tp = look([t[1] for t in OWN], n)
        tally(whole, ROWS, lambda k: 2 * tp + k, scores(whole, text_of(tp)))
        return carry

    def chain(*items):
        ahead = scores(items[0][0], items[0][3]())
        for k, (ri, m, cols, _) in enumerate(items):
            here = ahead
            if k + 1 < len(items):
                ahead = scores(items[k + 1][0], items[k + 1][3]())
            tally(ri, m, cols, here)

    def panel(ri, m, tp):
        return (ri, m, lambda k: 2 * tp + k, lambda: text_of(tp))

    def mixed(ri, m, slot, odd):
        return (ri, m, lambda k: 6 * slot + odd + 4 * k, lambda: mixed_text(3 * slot, odd))

    def half_rows(code):
        return pl.ds(pl.multiple_of(ROWS + (code % 2) * MI, MI), MI)

    def half_tile(n, carry):
        code = look([t[1] for t in HALF], n)
        chain(panel(half_rows(code), MI, code // 2))
        return carry

    def wide(code):
        chain(*[panel(half_rows(code), MI, (code // 2) * 3 + u) for u in range(3)])

    def wide_tile(n, carry):
        wide(look([t[1] for t in WIDE], n))
        return carry

    most, other, final = pl.ds(0, ROWS + MI), pl.ds(ROWS, ROWS), pl.ds(ROWS + MI, MI)

    def early_tile(n, carry):
        chain(mixed(most, ROWS + MI, 3 + n, 0))
        return carry

    def last_tile(n, carry):
        chain(panel(final, MI, 10 + 3 * n), mixed(final, MI, 3 + n, 0),
              mixed(whole, ROWS, 3 + n, 1), mixed(other, ROWS, 3 + n, 1))
        return carry

    lax.fori_loop(0, 3, pair_tile, 0)
    posv[...] = jnp.sum(jnp.transpose(posr[...]), axis=0, keepdims=True)

    def within(q, lo, hi):
        return (q >= lo) & (q < hi)

    def slot(t, carry):
        q = t + T_AT

        @pl.when((x == 3) & within(q, NA + T_AHEAD, NQ))
        def _():
            c_t(q).start()

        q = t + LAST_AT

        @pl.when((x == 3) & within(q, NA, NQ))
        def _():
            arrived(A_R2, q, relay2.at[span(0, q)])
            c_e(q).start()
            c_f(q).start()

        early = within(t + 2, NA, NA + R_EARLY)
        q = jnp.where(x == 0, t - R0, jnp.where(x == 1, t - R1, jnp.where(x == 2, t - R2, jnp.where(early, t + 2, t - R3))))

        @pl.when(within(q, NA, NQ) & ((x < 3) | early | (q >= NA + R_EARLY)))
        def _():
            arrived(A_R, q, relay.at[span(0, q)])

            @pl.when(x == 1)
            def _():
                c_r1(q).start()

            @pl.when(x != 1)
            def _():
                c_r(q).start()

        q = t - 1 - first1

        @pl.when(within(q, 0, NQ))
        def _():
            arrived(A_A, q, txt.at[span(1, q)])

            @pl.when((q < NA) & (x < 3))
            def _():
                c_b(q).start()

            c_a2(q).start()

        @pl.when((x == 3) & within(t - C_B3, 0, NA))
        def _():
            c_b(t - C_B3).start()

        q = t - SECOND_AT

        @pl.when((x == 1) & within(q, NA, NQ))
        def _():
            arrived(A_R2, q, relay2.at[span(0, q)])
            c_d(q).start()

        def second(q):
            arrived(A_B, q, txt.at[span(3, q)])

            @pl.when(j == 1)
            def _():
                c_b2(q).start()

        @pl.when(within(t - B_AT, NA, NQ))
        def _():
            second(t - B_AT)

        @pl.when(within(t - 14, 0, NA))
        def _():
            second(t - 14)

        count = (t * PACE[0]) // PACE[1]
        q = count + AHEAD - 1

        @pl.when((count != ((t - 1) * PACE[0]) // PACE[1]) & within(q, AHEAD, NQ))
        def _():
            c_i(q).start()

        @pl.when((t == HALF_AT) | (t == ALL_AT))
        def _():
            def image(k, carry):
                arrived(A_I, k, img.at[span(1, k)])
                return carry
            half = (t // ALL_AT) * (NQ // 2)
            lax.fori_loop(half, half + NQ // 2, image, 0)

        @pl.when(within(t - 3, 0, NQ))
        def _():
            arrived(A_A2, t - 3, txt.at[span(2, t - 3)])

        @pl.when(within(t - 7, NA, NQ))
        def _():
            arrived(A_B2, t - 7, txt.at[span(4, t - 7)])

        @pl.when(within(t - 15, 0, NA))
        def _():
            arrived(A_B2, t - 15, txt.at[span(4, t - 15)])

        for tasks, tile in (
            (OWN, own_tile), (WIDE, wide_tile), (HALF, half_tile), (EARLY, early_tile), (LAST, last_tile),
        ):
            lax.fori_loop(look(upto(tasks), t - 1), look(upto(tasks), t), tile, 0)

        return carry

    lax.fori_loop(1, SLOTS + 1, slot, 0)

    def rows_of(part):
        ri = pl.ds(part * ROWS, ROWS)
        mt = jnp.transpose(rm[ri, :])
        st = jnp.transpose(rs[ri, :])
        top = jnp.max(mt, axis=0, keepdims=True)
        return top, jnp.sum(st * jnp.exp2(mt - top), axis=0, keepdims=True)

    def cols_of(slot, u):
        m = cm[slot * 6 + u]
        top = jnp.max(m, axis=0, keepdims=True)
        return top, jnp.sum(cs[slot * 6 + u] * jnp.exp2(m - top), axis=0, keepdims=True)

    def c_stat(k, to, dev):
        return pltpu.make_async_remote_copy(
            src_ref=stat_out.at[k], dst_ref=stat_in.at[to], send_sem=st_s.at[k], recv_sem=st_r.at[to],
            device_id=dev, device_id_type=MESH)

    def col_stats(slots):
        for k in slots:
            for u in range(6):
                top, total = cols_of(k, u)
                stat_out[k, 0:1, u * 128:(u + 1) * 128] = top
                stat_out[k, 1:2, u * 128:(u + 1) * 128] = total

    def far_sends(act):
        act(c_stat(3, 4, back2))

        @pl.when(j == 0)
        def _():
            act(c_stat(4, 3, mate2))

        @pl.when(j == 1)
        def _():
            act(c_stat(4, 1, other_core))

    def near_sends(act):
        act(c_stat(1, 2, nxt_from))

        @pl.when(j == 0)
        def _():
            act(c_stat(2, 1, mate1))

        @pl.when(j == 1)
        def _():
            act(c_stat(2, 3, mate1))

    col_stats((3, 4))
    far_sends(lambda c: c.start())

    def wide_rest(n, carry):
        wide(2 * n + 1)
        return carry

    lax.fori_loop(1, 3, wide_rest, 0)
    col_stats((1, 2))
    near_sends(lambda c: c.start())
    wide(1)
    top, total = rows_of(1)
    stat_out[0, 0:1, :] = top
    stat_out[0, 1:2, :] = total
    c_stat(0, 0, other_group).start()

    own_top, own_total = rows_of(0)
    mine = [cols_of(0, u) for u in range(6)]
    positive = posv[...]
    def sent(q, carry):
        c_i(q).wait_send()
        c_a2(q).wait_send()

        @pl.when((x < 3) | (q < NA))
        def _():
            c_a(q).wait_send()

        @pl.when(q < NA)
        def _():
            c_b(q).wait_send()

        @pl.when(q >= NA)
        def _():
            c_c(q).wait_send()
            c_r(q).wait_send()

        @pl.when((q >= NA) & (x % 2 == 1))
        def _():
            c_d(q).wait_send()

        @pl.when((q >= NA) & (x == 3))
        def _():
            c_f(q).wait_send()

        @pl.when(j == 0)
        def _():
            c_o(q).wait_send()

        @pl.when(j == 1)
        def _():
            c_b2(q).wait_send()

        return carry

    lax.fori_loop(0, NQ, sent, 0)

    for k in range(5):
        c_stat(0, k, other_core).wait_recv()
    in_top, in_total = stat_in[0, 0:1, :], stat_in[0, 1:2, :]
    m = jnp.maximum(own_top, in_top)
    total = own_total * jnp.exp2(own_top - m) + in_total * jnp.exp2(in_top - m)
    gaps[:ROWS] = (LN2 * (m - positive) + jnp.log(total)).reshape(ROWS)
    for u in range(6):
        ls = slice(u * 128, (u + 1) * 128)
        top, total = mine[u]
        m = top
        for k in range(1, 5):
            m = jnp.maximum(m, stat_in[k, 0:1, ls])
        total = total * jnp.exp2(top - m)
        for k in range(1, 5):
            total = total + stat_in[k, 1:2, ls] * jnp.exp2(stat_in[k, 0:1, ls] - m)
        pc = jnp.sum(posc[u // 2, :, u % 2 * 128:(u % 2 + 1) * 128], axis=0, keepdims=True)
        gaps[ROWS + u * 128:ROWS + (u + 1) * 128] = (LN2 * (m - pc) + jnp.log(total)).reshape(128)

    c_stat(0, 0, other_group).wait_send()
    far_sends(lambda c: c.wait_send())
    near_sends(lambda c: c.wait_send())


def per_device(image_features, text_features, logit_scale, pair_ids):
    vmem = pl.BlockSpec(memory_space=pltpu.VMEM)
    anywhere = pl.BlockSpec(memory_space=pl.ANY)
    out = jax.ShapeDtypeStruct((2 * ROWS,), jnp.float32)
    both = pl.pallas_call(
        kernel,
        out_shape=out,
        in_specs=[anywhere, anywhere, pl.BlockSpec(memory_space=pltpu.HBM), vmem],
        out_specs=vmem,
        scratch_shapes=[
            pltpu.VMEM((ROWS, D), jnp.bfloat16),
            pltpu.VMEM((ROWS, D), jnp.bfloat16),
            pltpu.VMEM((2 * ROWS, D), jnp.bfloat16),
            pltpu.VMEM((5 * ROWS, D), jnp.bfloat16),
            pltpu.VMEM((ROWS, D), jnp.bfloat16),
            pltpu.VMEM((ROWS, D), jnp.bfloat16),
            pltpu.VMEM((2 * ROWS, 128), jnp.float32),
            pltpu.VMEM((2 * ROWS, 128), jnp.float32),
            pltpu.VMEM((30, 8, 128), jnp.float32),
            pltpu.VMEM((30, 8, 128), jnp.float32),
            pltpu.VMEM((ROWS, 128), jnp.float32),
            pltpu.VMEM((3, 8, NT), jnp.float32),
            pltpu.VMEM((ROWS, 128), jnp.float32),
            pltpu.VMEM((1, ROWS), jnp.float32),
            pltpu.VMEM((5, 8, ROWS), jnp.float32),
            pltpu.VMEM((5, 8, ROWS), jnp.float32),
            pltpu.SemaphoreType.DMA((10, NQ)),
            pltpu.SemaphoreType.DMA((7, NQ)),
            pltpu.SemaphoreType.DMA((2, ROWS // PART)),
            pltpu.SemaphoreType.DMA((5,)),
            pltpu.SemaphoreType.DMA((5,)),
            pltpu.SMEM((1,), jnp.float32),
            pltpu.SemaphoreType.DMA,
        ],
        compiler_params=pltpu.CompilerParams(
            collective_id=0, has_side_effects=True, vmem_limit_bytes=56 * 2**20),
        cost_estimate=pl.CostEstimate(flops=15 * 10**9, bytes_accessed=4 * 10**6, transcendentals=12 * 10**6),
    )(image_features, text_features, logit_scale, pair_ids)
    return both[:ROWS], both[ROWS:]


def solution(mesh):
    placed = (P(("group", "blk"), None), P(("group", "blk"), None), P(), P(("group", "blk")))
    return jax.shard_map(
        per_device,
        mesh=mesh,
        in_specs=placed,
        out_specs=(P(("group", "blk")), P(("group", "blk"))),
        check_vma=False,
    )
```

```python
import math

import jax
import jax.numpy as jnp
from jax import lax
from jax.experimental import pallas as pl
from jax.experimental.pallas import tpu as pltpu
from jax.sharding import PartitionSpec as P

MESH = pl.DeviceIdType.MESH
ROWS = 768
D = 1280
NBLK = 64
Q = 64
NQ = ROWS // Q
PART = 192
NA = 4
MI = 384
AHEAD = 2
SLOTS = 18
PACE = (3, 4)
HALF_AT, ALL_AT = 11, 17
T_AHEAD = 5
T_AT = 8
LAST_AT = 1
R0, R1, R2 = 0, 0, 3
R_EARLY, R3 = 5, 4
SECOND_AT = 4
B_AT = 6
C_B3 = 10
NT = 256
LOG2E = math.log2(math.e)
LN2 = math.log(2.0)
LOW = -1e30

K_I, K_A, K_C, K_O, K_A2, K_B, K_R, K_R2, K_R2B, K_B2 = range(10)
A_I, A_A, A_A2, A_B, A_B2, A_R, A_R2 = range(7)


OWN = [(5, 3), (6, 6), (9, 4), (10, 7), (13, 5), (13, 10), (14, 8), (14, 13)]
HALF = [(13, 20), (14, 26)]
WIDE = [(HALF_AT, 0), (13, 2), (14, 4)]
EARLY = [(15, 0), (16, 1)]
LAST = [(17, 0), (18, 1)]


def look(values, n):
    words = [sum(v << (6 * k) for k, v in enumerate(values[i:i + 5])) for i in range(0, len(values), 5)]
    word = words[0]
    for i in range(1, len(words)):
        word = jnp.where(n // 5 == i, words[i], word)
    return (word // (1 << (6 * (n % 5)))) % 64


def upto(tasks):
    return [sum(t[0] <= k for t in tasks) for k in range(SLOTS + 1)]


def kernel(img_hbm, txt_hbm, scale_hbm, pair_ref, gaps,
           raw_i, raw_t, img, txt, relay, relay2, rm, rs, cm, cs, posr, posc, loc, posv,
           stat_out, stat_in, ss, rsem, lsem, st_s, st_r, scale_ref, scale_sem):
    g = lax.axis_index("group")
    b = lax.axis_index("blk")
    j = b % 2
    x = (b // 2) % 4
    wrap3 = x // 3
    wrap2 = x // 2
    first1 = 1 - (x + 2) // 3
    first2 = 1 - x // 2

    def at(group, blk):
        return (group % 2, (blk + 2 * NBLK) % NBLK)

    row0 = b - 2 * x
    other_group = at(g + 1, b)
    other_core = at(g, b + 1 - 2 * j)
    nxt = at(g + j * wrap3, b + 2)
    nxt_from = at(g + j * first1, b - 2)
    xprev = at(g, row0 + 2 * ((x + 3) % 4))
    xprev_from = at(g, row0 + 2 * ((x + 1) % 4))
    row_next = at(g + j, b + 8)
    row_prev = at(g + j, b - 8)
    row_first = at(g, row0)
    row_last = at(g, row0 + 6)
    mate1 = at(g + (1 - j) * first1, b - 2 + 1 - 2 * j)
    mate1_from = at(g + j * wrap3, b + 2 + 1 - 2 * j)
    back2 = at(g + j * first2, b - 4)
    back2_from = at(g + j * wrap2, b + 4)
    mate2 = at(g + first2, b - 3)
    mate2_from = at(g + wrap2, b + 3)

    def fetch(kind, n):
        sl = pl.ds(pl.multiple_of(n * PART, PART), PART)
        src, dst = ((txt_hbm, raw_t), (img_hbm, raw_i))[kind]
        return pltpu.make_async_copy(src.at[sl], dst.at[sl], lsem.at[kind, n])

    fetch(0, 0).start()

    barrier = pltpu.get_barrier_semaphore()

    def hello(dev):
        pl.semaphore_signal(barrier, inc=1, device_id=dev, device_id_type=MESH)

    hello(nxt)
    hello(nxt_from)
    hello(mate1_from)
    hello(back2_from)

    @pl.when(j == 1)
    def _():
        hello(mate2_from)

    @pl.when(x % 2 == 1)
    def _():
        hello(row_prev)

    hello(other_group)
    hello(xprev_from)

    @pl.when(x == 0)
    def _():
        hello(row_last)

    hello(other_core)

    get_scale = pltpu.make_async_copy(scale_hbm, scale_ref, scale_sem)
    get_scale.start()

    for kind in range(2):
        for n in range(1 - kind, ROWS // PART):
            fetch(kind, n).start()

    pl.semaphore_wait(barrier, 7 + x % 2 + wrap3 + 1 - j)

    def span(slot, q):
        return pl.ds(pl.multiple_of(slot * ROWS + q * Q, Q), Q)

    def push(kind, arrival, q, src, dst, dev):
        return pltpu.make_async_remote_copy(
            src_ref=src, dst_ref=dst, send_sem=ss.at[kind, q], recv_sem=rsem.at[arrival, q],
            device_id=dev, device_id_type=MESH)

    def arrived(arrival, q, dst):
        push(K_I, arrival, q, dst, dst, other_core).wait_recv()

    def c_i(q):
        return push(K_I, A_I, q, img.at[span(0, q)], img.at[span(1, q)], other_group)

    def c_a(q):
        return push(K_A, A_A, q, txt.at[span(0, q)], txt.at[span(1, q)], nxt)

    def c_c(q):
        return push(K_C, A_R, q, txt.at[span(0, q)], relay.at[span(0, q)], xprev)

    def c_t(q):
        return push(K_C, A_R2, q, txt.at[span(0, q)], relay2.at[span(0, q)], row_next)

    def c_o(q):
        return push(K_O, A_B2, q, txt.at[span(0, q)], txt.at[span(4, q)], other_core)

    def c_a2(q):
        return push(K_A2, A_A2, q, txt.at[span(1, q)], txt.at[span(2, q)], other_core)

    def c_b(q):
        return push(K_B, A_B, q, txt.at[span(1, q)], txt.at[span(3, q)], nxt)

    def c_r(q):
        return push(K_R, A_B, q, relay.at[span(0, q)], txt.at[span(3, q)], xprev)

    def c_r1(q):
        return push(K_R, A_R2, q, relay.at[span(0, q)], relay2.at[span(0, q)], row_next)

    def c_d(q):
        return push(K_R2, A_B, q, relay2.at[span(0, q)], txt.at[span(3, q)], xprev)

    def c_e(q):
        return push(K_R2, A_A, q, relay2.at[span(0, q)], txt.at[span(1, q)], row_first)

    def c_f(q):
        return push(K_R2B, A_R, q, relay2.at[span(0, q)], relay.at[span(0, q)], xprev)

    def c_b2(q):
        return push(K_B2, A_B2, q, txt.at[span(3, q)], txt.at[span(4, q)], other_core)

    def unit(raw):
        wide = raw.astype(jnp.float32)
        inverse = lax.rsqrt(jnp.mean(wide * wide, axis=-1, keepdims=True) + 1e-06)
        return (wide * inverse * D ** (-0.5)).astype(jnp.bfloat16)

    def own_text(n, carry):
        q = n
        sl = span(0, q)
        @pl.when(q % (PART // Q) == 0)
        def _():
            fetch(0, q // (PART // Q)).wait()

        txt[sl, :] = unit(raw_t[sl, :])

        @pl.when((x < 3) | (q < NA))
        def _():
            c_a(q).start()

        @pl.when((x < 3) & (q >= NA))
        def _():
            c_c(q).start()

        @pl.when((x == 3) & (q >= NA) & (q < NA + T_AHEAD))
        def _():
            c_t(q).start()

        @pl.when(j == 0)
        def _():
            c_o(q).start()

        return carry

    def own_image(q, carry):
        sl = span(0, q)

        @pl.when(q % (PART // Q) == 0)
        def _():
            fetch(1, q // (PART // Q)).wait()

        img[sl, :] = unit(raw_i[sl, :])

        @pl.when(q < AHEAD)
        def _():
            c_i(q).start()

        return carry

    lax.fori_loop(0, NQ, own_text, 0)
    lax.fori_loop(0, NQ, own_image, 0)

    rm[...] = jnp.full_like(rm, LOW)
    rs[...] = jnp.zeros_like(rs)
    cm[...] = jnp.full_like(cm, LOW)
    cs[...] = jnp.zeros_like(cs)
    posr[...] = jnp.zeros_like(posr)
    posc[...] = jnp.zeros_like(posc)
    base = (g * NBLK + b) * ROWS
    ids = (pair_ref[...] - base).astype(jnp.float32).reshape(1, ROWS)
    loc[...] = jnp.transpose(jnp.broadcast_to(ids, (128, ROWS)))

    get_scale.wait()
    sc = scale_ref[0] * LOG2E

    def mixed_text(tp, odd):
        at0 = pl.multiple_of(tp * NT + odd * 128, 128)
        return jnp.concatenate([txt[pl.ds(at0, 128), :], txt[pl.ds(at0 + 2 * NT, 128), :]], axis=0)

    def text_of(tp):
        return txt[pl.ds(pl.multiple_of(tp * NT, NT), NT), :]

    def scores(ri, text):
        return lax.dot_general(
            img[ri, :], text, (((1,), (1,)), ((), ())), preferred_element_type=jnp.float32) * sc

    def tally(ri, m, cols, s):
        n = s.shape[1] // 128
        parts = [s[:, k * 128:(k + 1) * 128] for k in range(n)]
        ro = rm[ri, :]
        rn = ro
        for part in parts:
            rn = jnp.maximum(rn, part)
        total = rs[ri, :] * jnp.exp2(ro - rn)
        for part in parts:
            total = total + jnp.exp2(part - rn)
        rs[ri, :] = total
        rm[ri, :] = rn
        for k in range(n):
            c = cols(k)
            s3 = parts[k].reshape(m // 8, 8, 128)
            co = cm[c]
            cn = jnp.maximum(co, jnp.max(s3, axis=0))
            cs[c] = cs[c] * jnp.exp2(co - cn) + jnp.sum(jnp.exp2(s3 - cn[None]), axis=0)
            cm[c] = cn

    whole = pl.ds(0, ROWS)

    def pair_tile(tp, carry):
        s = scores(whole, text_of(tp))
        lane = (lax.broadcasted_iota(jnp.int32, (ROWS, 128), 1) + tp * NT).astype(jnp.float32)
        want = loc[...]
        left = jnp.where(want == lane, s[:, :128], 0.0)
        right = jnp.where(want == lane + 128.0, s[:, 128:], 0.0)
        posr[...] = posr[...] + (left + right)
        posc[tp, :, :128] = jnp.sum(left.reshape(ROWS // 8, 8, 128), axis=0)
        posc[tp, :, 128:] = jnp.sum(right.reshape(ROWS // 8, 8, 128), axis=0)
        tally(whole, ROWS, lambda k: 2 * tp + k, s)
        return carry

    def own_tile(n, carry):
        tp = look([t[1] for t in OWN], n)
        tally(whole, ROWS, lambda k: 2 * tp + k, scores(whole, text_of(tp)))
        return carry

    def chain(*items):
        ahead = scores(items[0][0], items[0][3]())
        for k, (ri, m, cols, _) in enumerate(items):
            here = ahead
            if k + 1 < len(items):
                ahead = scores(items[k + 1][0], items[k + 1][3]())
            tally(ri, m, cols, here)

    def panel(ri, m, tp):
        return (ri, m, lambda k: 2 * tp + k, lambda: text_of(tp))

    def mixed(ri, m, slot, odd):
        return (ri, m, lambda k: 6 * slot + odd + 4 * k, lambda: mixed_text(3 * slot, odd))

    def half_rows(code):
        return pl.ds(pl.multiple_of(ROWS + (code % 2) * MI, MI), MI)

    def half_tile(n, carry):
        code = look([t[1] for t in HALF], n)
        chain(panel(half_rows(code), MI, code // 2))
        return carry

    def wide(code):
        chain(*[panel(half_rows(code), MI, (code // 2) * 3 + u) for u in range(3)])

    def wide_tile(n, carry):
        wide(look([t[1] for t in WIDE], n))
        return carry

    most, other, final = pl.ds(0, ROWS + MI), pl.ds(ROWS, ROWS), pl.ds(ROWS + MI, MI)

    def early_tile(n, carry):
        chain(mixed(most, ROWS + MI, 3 + n, 0))
        return carry

    def last_tile(n, carry):
        chain(panel(final, MI, 10 + 3 * n), mixed(final, MI, 3 + n, 0),
              *[mixed(pl.ds(h * MI, MI), MI, 3 + n, 1) for h in range(4)])
        return carry

    lax.fori_loop(0, 3, pair_tile, 0)
    posv[...] = jnp.sum(jnp.transpose(posr[...]), axis=0, keepdims=True)

    def within(q, lo, hi):
        return (q >= lo) & (q < hi)

    def slot(t, carry):
        q = t + T_AT

        @pl.when((x == 3) & within(q, NA + T_AHEAD, NQ))
        def _():
            c_t(q).start()

        q = t + LAST_AT

        @pl.when((x == 3) & within(q, NA, NQ))
        def _():
            arrived(A_R2, q, relay2.at[span(0, q)])
            c_e(q).start()
            c_f(q).start()

        early = within(t + 2, NA, NA + R_EARLY)
        q = jnp.where(x == 0, t - R0, jnp.where(x == 1, t - R1, jnp.where(x == 2, t - R2, jnp.where(early, t + 2, t - R3))))

        @pl.when(within(q, NA, NQ) & ((x < 3) | early | (q >= NA + R_EARLY)))
        def _():
            arrived(A_R, q, relay.at[span(0, q)])

            @pl.when(x == 1)
            def _():
                c_r1(q).start()

            @pl.when(x != 1)
            def _():
                c_r(q).start()

        q = t - 1 - first1

        @pl.when(within(q, 0, NQ))
        def _():
            arrived(A_A, q, txt.at[span(1, q)])

            @pl.when((q < NA) & (x < 3))
            def _():
                c_b(q).start()

            c_a2(q).start()

        @pl.when((x == 3) & within(t - C_B3, 0, NA))
        def _():
            c_b(t - C_B3).start()

        q = t - SECOND_AT

        @pl.when((x == 1) & within(q, NA, NQ))
        def _():
            arrived(A_R2, q, relay2.at[span(0, q)])
            c_d(q).start()

        def second(q):
            arrived(A_B, q, txt.at[span(3, q)])

            @pl.when(j == 1)
            def _():
                c_b2(q).start()

        @pl.when(within(t - B_AT, NA, NQ))
        def _():
            second(t - B_AT)

        @pl.when(within(t - 14, 0, NA))
        def _():
            second(t - 14)

        count = (t * PACE[0]) // PACE[1]
        q = count + AHEAD - 1

        @pl.when((count != ((t - 1) * PACE[0]) // PACE[1]) & within(q, AHEAD, NQ))
        def _():
            c_i(q).start()

        @pl.when((t == HALF_AT) | (t == ALL_AT))
        def _():
            def image(k, carry):
                arrived(A_I, k, img.at[span(1, k)])
                return carry
            half = (t // ALL_AT) * (NQ // 2)
            lax.fori_loop(half, half + NQ // 2, image, 0)

        @pl.when(within(t - 3, 0, NQ))
        def _():
            arrived(A_A2, t - 3, txt.at[span(2, t - 3)])

        @pl.when(within(t - 7, NA, NQ))
        def _():
            arrived(A_B2, t - 7, txt.at[span(4, t - 7)])

        @pl.when(within(t - 15, 0, NA))
        def _():
            arrived(A_B2, t - 15, txt.at[span(4, t - 15)])

        for tasks, tile in (
            (OWN, own_tile), (WIDE, wide_tile), (HALF, half_tile), (EARLY, early_tile), (LAST, last_tile),
        ):
            lax.fori_loop(look(upto(tasks), t - 1), look(upto(tasks), t), tile, 0)

        return carry

    lax.fori_loop(1, SLOTS + 1, slot, 0)

    def rows_of(part):
        ri = pl.ds(part * ROWS, ROWS)
        mt = jnp.transpose(rm[ri, :])
        st = jnp.transpose(rs[ri, :])
        top = jnp.max(mt, axis=0, keepdims=True)
        return top, jnp.sum(st * jnp.exp2(mt - top), axis=0, keepdims=True)

    def cols_of(slot, u):
        m = cm[slot * 6 + u]
        top = jnp.max(m, axis=0, keepdims=True)
        return top, jnp.sum(cs[slot * 6 + u] * jnp.exp2(m - top), axis=0, keepdims=True)

    def c_stat(k, to, dev):
        return pltpu.make_async_remote_copy(
            src_ref=stat_out.at[k], dst_ref=stat_in.at[to], send_sem=st_s.at[k], recv_sem=st_r.at[to],
            device_id=dev, device_id_type=MESH)

    def col_stats(slots):
        for k in slots:
            for u in range(6):
                top, total = cols_of(k, u)
                stat_out[k, 0:1, u * 128:(u + 1) * 128] = top
                stat_out[k, 1:2, u * 128:(u + 1) * 128] = total

    def far_sends(act):
        act(c_stat(3, 4, back2))

        @pl.when(j == 0)
        def _():
            act(c_stat(4, 3, mate2))

        @pl.when(j == 1)
        def _():
            act(c_stat(4, 1, other_core))

    def near_sends(act):
        act(c_stat(1, 2, nxt_from))

        @pl.when(j == 0)
        def _():
            act(c_stat(2, 1, mate1))

        @pl.when(j == 1)
        def _():
            act(c_stat(2, 3, mate1))

    col_stats((3, 4))
    far_sends(lambda c: c.start())

    def wide_rest(n, carry):
        wide(2 * n + 1)
        return carry

    lax.fori_loop(1, 3, wide_rest, 0)
    col_stats((1, 2))
    near_sends(lambda c: c.start())
    wide(1)
    top, total = rows_of(1)
    stat_out[0, 0:1, :] = top
    stat_out[0, 1:2, :] = total
    c_stat(0, 0, other_group).start()

    own_top, own_total = rows_of(0)
    mine = [cols_of(0, u) for u in range(6)]
    positive = posv[...]
    def sent(q, carry):
        c_i(q).wait_send()
        c_a2(q).wait_send()

        @pl.when((x < 3) | (q < NA))
        def _():
            c_a(q).wait_send()

        @pl.when(q < NA)
        def _():
            c_b(q).wait_send()

        @pl.when(q >= NA)
        def _():
            c_c(q).wait_send()
            c_r(q).wait_send()

        @pl.when((q >= NA) & (x % 2 == 1))
        def _():
            c_d(q).wait_send()

        @pl.when((q >= NA) & (x == 3))
        def _():
            c_f(q).wait_send()

        @pl.when(j == 0)
        def _():
            c_o(q).wait_send()

        @pl.when(j == 1)
        def _():
            c_b2(q).wait_send()

        return carry

    lax.fori_loop(0, NQ, sent, 0)

    for k in range(5):
        c_stat(0, k, other_core).wait_recv()
    in_top, in_total = stat_in[0, 0:1, :], stat_in[0, 1:2, :]
    m = jnp.maximum(own_top, in_top)
    total = own_total * jnp.exp2(own_top - m) + in_total * jnp.exp2(in_top - m)
    gaps[:ROWS] = (LN2 * (m - positive) + jnp.log(total)).reshape(ROWS)
    for u in range(6):
        ls = slice(u * 128, (u + 1) * 128)
        top, total = mine[u]
        m = top
        for k in range(1, 5):
            m = jnp.maximum(m, stat_in[k, 0:1, ls])
        total = total * jnp.exp2(top - m)
        for k in range(1, 5):
            total = total + stat_in[k, 1:2, ls] * jnp.exp2(stat_in[k, 0:1, ls] - m)
        pc = jnp.sum(posc[u // 2, :, u % 2 * 128:(u % 2 + 1) * 128], axis=0, keepdims=True)
        gaps[ROWS + u * 128:ROWS + (u + 1) * 128] = (LN2 * (m - pc) + jnp.log(total)).reshape(128)

    c_stat(0, 0, other_group).wait_send()
    far_sends(lambda c: c.wait_send())
    near_sends(lambda c: c.wait_send())


def per_device(image_features, text_features, logit_scale, pair_ids):
    vmem = pl.BlockSpec(memory_space=pltpu.VMEM)
    anywhere = pl.BlockSpec(memory_space=pl.ANY)
    out = jax.ShapeDtypeStruct((2 * ROWS,), jnp.float32)
    both = pl.pallas_call(
        kernel,
        out_shape=out,
        in_specs=[anywhere, anywhere, pl.BlockSpec(memory_space=pltpu.HBM), vmem],
        out_specs=vmem,
        scratch_shapes=[
            pltpu.VMEM((ROWS, D), jnp.bfloat16),
            pltpu.VMEM((ROWS, D), jnp.bfloat16),
            pltpu.VMEM((2 * ROWS, D), jnp.bfloat16),
            pltpu.VMEM((5 * ROWS, D), jnp.bfloat16),
            pltpu.VMEM((ROWS, D), jnp.bfloat16),
            pltpu.VMEM((ROWS, D), jnp.bfloat16),
            pltpu.VMEM((2 * ROWS, 128), jnp.float32),
            pltpu.VMEM((2 * ROWS, 128), jnp.float32),
            pltpu.VMEM((30, 8, 128), jnp.float32),
            pltpu.VMEM((30, 8, 128), jnp.float32),
            pltpu.VMEM((ROWS, 128), jnp.float32),
            pltpu.VMEM((3, 8, NT), jnp.float32),
            pltpu.VMEM((ROWS, 128), jnp.float32),
            pltpu.VMEM((1, ROWS), jnp.float32),
            pltpu.VMEM((5, 8, ROWS), jnp.float32),
            pltpu.VMEM((5, 8, ROWS), jnp.float32),
            pltpu.SemaphoreType.DMA((10, NQ)),
            pltpu.SemaphoreType.DMA((7, NQ)),
            pltpu.SemaphoreType.DMA((2, ROWS // PART)),
            pltpu.SemaphoreType.DMA((5,)),
            pltpu.SemaphoreType.DMA((5,)),
            pltpu.SMEM((1,), jnp.float32),
            pltpu.SemaphoreType.DMA,
        ],
        compiler_params=pltpu.CompilerParams(
            collective_id=0, has_side_effects=True, vmem_limit_bytes=56 * 2**20),
        cost_estimate=pl.CostEstimate(flops=15 * 10**9, bytes_accessed=4 * 10**6, transcendentals=12 * 10**6),
    )(image_features, text_features, logit_scale, pair_ids)
    return both[:ROWS], both[ROWS:]


def solution(mesh):
    placed = (P(("group", "blk"), None), P(("group", "blk"), None), P(), P(("group", "blk")))
    return jax.shard_map(
        per_device,
        mesh=mesh,
        in_specs=placed,
        out_specs=(P(("group", "blk")), P(("group", "blk"))),
        check_vma=False,
    )
```

```python
import math

import jax
import jax.numpy as jnp
from jax import lax
from jax.experimental import pallas as pl
from jax.experimental.pallas import tpu as pltpu
from jax.sharding import PartitionSpec as P

MESH = pl.DeviceIdType.MESH
ROWS = 768
D = 1280
NBLK = 64
Q = 64
NQ = ROWS // Q
PART = 192
NA = 4
MI = 384
AHEAD = 2
SLOTS = 18
PACE = (3, 4)
HALF_AT, ALL_AT = 11, 17
T_AHEAD = 5
T_AT = 8
LAST_AT = 1
R0, R1, R2 = 0, 0, 3
R_EARLY, R3 = 5, 4
SECOND_AT = 4
B_AT = 6
C_B3 = 10
NT = 256
LOG2E = math.log2(math.e)
LN2 = math.log(2.0)
LOW = -1e30

K_I, K_A, K_C, K_O, K_A2, K_B, K_R, K_R2, K_R2B, K_B2 = range(10)
A_I, A_A, A_A2, A_B, A_B2, A_R, A_R2 = range(7)


OWN = [(5, 3), (6, 6), (9, 4), (10, 7), (13, 5), (13, 10), (14, 8), (14, 13)]
HALF = [(13, 20), (14, 26)]
WIDE = [(HALF_AT, 0), (13, 2), (14, 4)]
EARLY = [(15, 0), (16, 1)]
LAST = [(17, 0), (18, 1)]


def look(values, n):
    words = [sum(v << (6 * k) for k, v in enumerate(values[i:i + 5])) for i in range(0, len(values), 5)]
    word = words[0]
    for i in range(1, len(words)):
        word = jnp.where(n // 5 == i, words[i], word)
    return (word // (1 << (6 * (n % 5)))) % 64


def upto(tasks):
    return [sum(t[0] <= k for t in tasks) for k in range(SLOTS + 1)]


def kernel(img_hbm, txt_hbm, scale_hbm, pair_ref, gaps,
           raw_i, raw_t, img, txt, relay, relay2, rm, rs, cm, cs, posr, posc, loc, posv,
           stat_out, stat_in, ss, rsem, lsem, st_s, st_r, scale_ref, scale_sem):
    g = lax.axis_index("group")
    b = lax.axis_index("blk")
    j = b % 2
    x = (b // 2) % 4
    wrap3 = x // 3
    wrap2 = x // 2
    first1 = 1 - (x + 2) // 3
    first2 = 1 - x // 2

    def at(group, blk):
        return (group % 2, (blk + 2 * NBLK) % NBLK)

    row0 = b - 2 * x
    other_group = at(g + 1, b)
    other_core = at(g, b + 1 - 2 * j)
    nxt = at(g + j * wrap3, b + 2)
    nxt_from = at(g + j * first1, b - 2)
    xprev = at(g, row0 + 2 * ((x + 3) % 4))
    xprev_from = at(g, row0 + 2 * ((x + 1) % 4))
    row_next = at(g + j, b + 8)
    row_prev = at(g + j, b - 8)
    row_first = at(g, row0)
    row_last = at(g, row0 + 6)
    mate1 = at(g + (1 - j) * first1, b - 2 + 1 - 2 * j)
    mate1_from = at(g + j * wrap3, b + 2 + 1 - 2 * j)
    back2 = at(g + j * first2, b - 4)
    back2_from = at(g + j * wrap2, b + 4)
    mate2 = at(g + first2, b - 3)
    mate2_from = at(g + wrap2, b + 3)

    def fetch(kind, n):
        sl = pl.ds(pl.multiple_of(n * PART, PART), PART)
        src, dst = ((txt_hbm, raw_t), (img_hbm, raw_i))[kind]
        return pltpu.make_async_copy(src.at[sl], dst.at[sl], lsem.at[kind, n])

    fetch(0, 0).start()

    barrier = pltpu.get_barrier_semaphore()

    def hello(dev):
        pl.semaphore_signal(barrier, inc=1, device_id=dev, device_id_type=MESH)

    hello(nxt)
    hello(nxt_from)
    hello(mate1_from)
    hello(back2_from)

    @pl.when(j == 1)
    def _():
        hello(mate2_from)

    @pl.when(x % 2 == 1)
    def _():
        hello(row_prev)

    hello(other_group)
    hello(xprev_from)

    @pl.when(x == 0)
    def _():
        hello(row_last)

    hello(other_core)

    get_scale = pltpu.make_async_copy(scale_hbm, scale_ref, scale_sem)
    get_scale.start()

    for kind in range(2):
        for n in range(1 - kind, ROWS // PART):
            fetch(kind, n).start()

    pl.semaphore_wait(barrier, 7 + x % 2 + wrap3 + 1 - j)

    def span(slot, q):
        return pl.ds(pl.multiple_of(slot * ROWS + q * Q, Q), Q)

    def push(kind, arrival, q, src, dst, dev):
        return pltpu.make_async_remote_copy(
            src_ref=src, dst_ref=dst, send_sem=ss.at[kind, q], recv_sem=rsem.at[arrival, q],
            device_id=dev, device_id_type=MESH)

    def arrived(arrival, q, dst):
        push(K_I, arrival, q, dst, dst, other_core).wait_recv()

    def c_i(q):
        return push(K_I, A_I, q, img.at[span(0, q)], img.at[span(1, q)], other_group)

    def c_a(q):
        return push(K_A, A_A, q, txt.at[span(0, q)], txt.at[span(1, q)], nxt)

    def c_c(q):
        return push(K_C, A_R, q, txt.at[span(0, q)], relay.at[span(0, q)], xprev)

    def c_t(q):
        return push(K_C, A_R2, q, txt.at[span(0, q)], relay2.at[span(0, q)], row_next)

    def c_o(q):
        return push(K_O, A_B2, q, txt.at[span(0, q)], txt.at[span(4, q)], other_core)

    def c_a2(q):
        return push(K_A2, A_A2, q, txt.at[span(1, q)], txt.at[span(2, q)], other_core)

    def c_b(q):
        return push(K_B, A_B, q, txt.at[span(1, q)], txt.at[span(3, q)], nxt)

    def c_r(q):
        return push(K_R, A_B, q, relay.at[span(0, q)], txt.at[span(3, q)], xprev)

    def c_r1(q):
        return push(K_R, A_R2, q, relay.at[span(0, q)], relay2.at[span(0, q)], row_next)

    def c_d(q):
        return push(K_R2, A_B, q, relay2.at[span(0, q)], txt.at[span(3, q)], xprev)

    def c_e(q):
        return push(K_R2, A_A, q, relay2.at[span(0, q)], txt.at[span(1, q)], row_first)

    def c_f(q):
        return push(K_R2B, A_R, q, relay2.at[span(0, q)], relay.at[span(0, q)], xprev)

    def c_b2(q):
        return push(K_B2, A_B2, q, txt.at[span(3, q)], txt.at[span(4, q)], other_core)

    def unit(raw):
        wide = raw.astype(jnp.float32)
        inverse = lax.rsqrt(jnp.mean(wide * wide, axis=-1, keepdims=True) + 1e-06)
        return (wide * inverse * D ** (-0.5)).astype(jnp.bfloat16)

    def own_text(n, carry):
        q = n
        sl = span(0, q)
        @pl.when(q % (PART // Q) == 0)
        def _():
            fetch(0, q // (PART // Q)).wait()

        txt[sl, :] = unit(raw_t[sl, :])

        @pl.when((x < 3) | (q < NA))
        def _():
            c_a(q).start()

        @pl.when((x < 3) & (q >= NA))
        def _():
            c_c(q).start()

        @pl.when((x == 3) & (q >= NA) & (q < NA + T_AHEAD))
        def _():
            c_t(q).start()

        @pl.when(j == 0)
        def _():
            c_o(q).start()

        return carry

    def own_image(q, carry):
        sl = span(0, q)

        @pl.when(q % (PART // Q) == 0)
        def _():
            fetch(1, q // (PART // Q)).wait()

        img[sl, :] = unit(raw_i[sl, :])

        @pl.when(q < AHEAD)
        def _():
            c_i(q).start()

        return carry

    lax.fori_loop(0, NQ, own_text, 0)
    lax.fori_loop(0, NQ, own_image, 0)

    rm[...] = jnp.full_like(rm, LOW)
    rs[...] = jnp.zeros_like(rs)
    cm[...] = jnp.full_like(cm, LOW)
    cs[...] = jnp.zeros_like(cs)
    posr[...] = jnp.zeros_like(posr)
    posc[...] = jnp.zeros_like(posc)
    base = (g * NBLK + b) * ROWS
    ids = (pair_ref[...] - base).astype(jnp.float32).reshape(1, ROWS)
    loc[...] = jnp.transpose(jnp.broadcast_to(ids, (128, ROWS)))

    get_scale.wait()
    sc = scale_ref[0] * LOG2E

    def mixed_text(tp, odd):
        at0 = pl.multiple_of(tp * NT + odd * 128, 128)
        return jnp.concatenate([txt[pl.ds(at0, 128), :], txt[pl.ds(at0 + 2 * NT, 128), :]], axis=0)

    def text_of(tp):
        return txt[pl.ds(pl.multiple_of(tp * NT, NT), NT), :]

    def scores(ri, text):
        return lax.dot_general(
            img[ri, :], text, (((1,), (1,)), ((), ())), preferred_element_type=jnp.float32) * sc

    def tally(ri, m, cols, s):
        n = s.shape[1] // 128
        parts = [s[:, k * 128:(k + 1) * 128] for k in range(n)]
        ro = rm[ri, :]
        rn = ro
        for part in parts:
            rn = jnp.maximum(rn, part)
        total = rs[ri, :] * jnp.exp2(ro - rn)
        for part in parts:
            total = total + jnp.exp2(part - rn)
        rs[ri, :] = total
        rm[ri, :] = rn
        for k in range(n):
            c = cols(k)
            s3 = parts[k].reshape(m // 8, 8, 128)
            co = cm[c]
            cn = jnp.maximum(co, jnp.max(s3, axis=0))
            cs[c] = cs[c] * jnp.exp2(co - cn) + jnp.sum(jnp.exp2(s3 - cn[None]), axis=0)
            cm[c] = cn

    whole = pl.ds(0, ROWS)

    def pair_tile(tp, carry):
        s = scores(whole, text_of(tp))
        lane = (lax.broadcasted_iota(jnp.int32, (ROWS, 128), 1) + tp * NT).astype(jnp.float32)
        want = loc[...]
        left = jnp.where(want == lane, s[:, :128], 0.0)
        right = jnp.where(want == lane + 128.0, s[:, 128:], 0.0)
        posr[...] = posr[...] + (left + right)
        posc[tp, :, :128] = jnp.sum(left.reshape(ROWS // 8, 8, 128), axis=0)
        posc[tp, :, 128:] = jnp.sum(right.reshape(ROWS // 8, 8, 128), axis=0)
        tally(whole, ROWS, lambda k: 2 * tp + k, s)
        return carry

    def own_tile(n, carry):
        tp = look([t[1] for t in OWN], n)
        tally(whole, ROWS, lambda k: 2 * tp + k, scores(whole, text_of(tp)))
        return carry

    def chain(*items):
        ahead = scores(items[0][0], items[0][3]())
        for k, (ri, m, cols, _) in enumerate(items):
            here = ahead
            if k + 1 < len(items):
                ahead = scores(items[k + 1][0], items[k + 1][3]())
            tally(ri, m, cols, here)

    def panel(ri, m, tp):
        return (ri, m, lambda k: 2 * tp + k, lambda: text_of(tp))

    def mixed(ri, m, slot, odd):
        return (ri, m, lambda k: 6 * slot + odd + 4 * k, lambda: mixed_text(3 * slot, odd))

    def half_rows(code):
        return pl.ds(pl.multiple_of(ROWS + (code % 2) * MI, MI), MI)

    def half_tile(n, carry):
        code = look([t[1] for t in HALF], n)
        chain(panel(half_rows(code), MI, code // 2))
        return carry

    def wide(code):
        chain(*[panel(half_rows(code), MI, (code // 2) * 3 + u) for u in range(3)])

    def wide_tile(n, carry):
        wide(look([t[1] for t in WIDE], n))
        return carry

    most, other, final = pl.ds(0, ROWS + MI), pl.ds(ROWS, ROWS), pl.ds(ROWS + MI, MI)

    def early_tile(n, carry):
        chain(mixed(most, ROWS + MI, 3 + n, 0))
        return carry

    def last_tile(n, carry):
        chain(panel(final, MI, 10 + 3 * n), mixed(final, MI, 3 + n, 0),
              *[mixed(pl.ds(h * MI, MI), MI, 3 + n, 1) for h in range(4)])
        return carry

    lax.fori_loop(0, 3, pair_tile, 0)
    posv[...] = jnp.sum(jnp.transpose(posr[...]), axis=0, keepdims=True)

    def within(q, lo, hi):
        return (q >= lo) & (q < hi)

    def slot(t, carry):
        q = t + T_AT

        @pl.when((x == 3) & within(q, NA + T_AHEAD, NQ))
        def _():
            c_t(q).start()

        q = t + LAST_AT

        @pl.when((x == 3) & within(q, NA, NQ))
        def _():
            arrived(A_R2, q, relay2.at[span(0, q)])
            c_e(q).start()
            c_f(q).start()

        early = within(t + 2, NA, NA + R_EARLY)
        q = jnp.where(x == 0, t - R0, jnp.where(x == 1, t - R1, jnp.where(x == 2, t - R2, jnp.where(early, t + 2, t - R3))))

        @pl.when(within(q, NA, NQ) & ((x < 3) | early | (q >= NA + R_EARLY)))
        def _():
            arrived(A_R, q, relay.at[span(0, q)])

            @pl.when(x == 1)
            def _():
                c_r1(q).start()

            @pl.when(x != 1)
            def _():
                c_r(q).start()

        q = t - 1 - first1

        @pl.when(within(q, 0, NQ))
        def _():
            arrived(A_A, q, txt.at[span(1, q)])

            @pl.when((q < NA) & (x < 3))
            def _():
                c_b(q).start()

            c_a2(q).start()

        @pl.when((x == 3) & within(t - C_B3, 0, NA))
        def _():
            c_b(t - C_B3).start()

        q = t - SECOND_AT

        @pl.when((x == 1) & within(q, NA, NQ))
        def _():
            arrived(A_R2, q, relay2.at[span(0, q)])
            c_d(q).start()

        def second(q):
            arrived(A_B, q, txt.at[span(3, q)])

            @pl.when(j == 1)
            def _():
                c_b2(q).start()

        @pl.when(within(t - B_AT, NA, NQ))
        def _():
            second(t - B_AT)

        @pl.when(within(t - 14, 0, NA))
        def _():
            second(t - 14)

        count = (t * PACE[0]) // PACE[1]
        q = count + AHEAD - 1

        @pl.when((count != ((t - 1) * PACE[0]) // PACE[1]) & within(q, AHEAD, NQ))
        def _():
            c_i(q).start()

        @pl.when((t == HALF_AT) | (t == ALL_AT))
        def _():
            def image(k, carry):
                arrived(A_I, k, img.at[span(1, k)])
                return carry
            half = (t // ALL_AT) * (NQ // 2)
            lax.fori_loop(half, half + NQ // 2, image, 0)

        @pl.when(within(t - 3, 0, NQ))
        def _():
            arrived(A_A2, t - 3, txt.at[span(2, t - 3)])

        @pl.when(within(t - 7, NA, NQ))
        def _():
            arrived(A_B2, t - 7, txt.at[span(4, t - 7)])

        @pl.when(within(t - 15, 0, NA))
        def _():
            arrived(A_B2, t - 15, txt.at[span(4, t - 15)])

        for tasks, tile in (
            (OWN, own_tile), (WIDE, wide_tile), (HALF, half_tile), (EARLY, early_tile), (LAST, last_tile),
        ):
            lax.fori_loop(look(upto(tasks), t - 1), look(upto(tasks), t), tile, 0)

        return carry

    lax.fori_loop(1, SLOTS + 1, slot, 0)

    def rows_of(part):
        ri = pl.ds(part * ROWS, ROWS)
        mt = jnp.transpose(rm[ri, :])
        st = jnp.transpose(rs[ri, :])
        top = jnp.max(mt, axis=0, keepdims=True)
        return top, jnp.sum(st * jnp.exp2(mt - top), axis=0, keepdims=True)

    def cols_of(slot, u):
        m = cm[slot * 6 + u]
        top = jnp.max(m, axis=0, keepdims=True)
        return top, jnp.sum(cs[slot * 6 + u] * jnp.exp2(m - top), axis=0, keepdims=True)

    def c_stat(k, to, dev):
        return pltpu.make_async_remote_copy(
            src_ref=stat_out.at[k], dst_ref=stat_in.at[to], send_sem=st_s.at[k], recv_sem=st_r.at[to],
            device_id=dev, device_id_type=MESH)

    def col_stats(slots):
        for k in slots:
            for u in range(6):
                top, total = cols_of(k, u)
                stat_out[k, 0:1, u * 128:(u + 1) * 128] = top
                stat_out[k, 1:2, u * 128:(u + 1) * 128] = total

    def far_sends(act):
        act(c_stat(3, 4, back2))

        @pl.when(j == 0)
        def _():
            act(c_stat(4, 3, mate2))

        @pl.when(j == 1)
        def _():
            act(c_stat(4, 1, other_core))

    def near_sends(act):
        act(c_stat(1, 2, nxt_from))

        @pl.when(j == 0)
        def _():
            act(c_stat(2, 1, mate1))

        @pl.when(j == 1)
        def _():
            act(c_stat(2, 3, mate1))

    col_stats((3, 4))
    far_sends(lambda c: c.start())

    chain(*[panel(final, MI, tp) for tp in range(3, 9)])
    col_stats((1, 2))
    near_sends(lambda c: c.start())
    wide(1)
    top, total = rows_of(1)
    stat_out[0, 0:1, :] = top
    stat_out[0, 1:2, :] = total
    c_stat(0, 0, other_group).start()

    own_top, own_total = rows_of(0)
    mine = [cols_of(0, u) for u in range(6)]
    positive = posv[...]
    def sent(q, carry):
        c_i(q).wait_send()
        c_a2(q).wait_send()

        @pl.when((x < 3) | (q < NA))
        def _():
            c_a(q).wait_send()

        @pl.when(q < NA)
        def _():
            c_b(q).wait_send()

        @pl.when(q >= NA)
        def _():
            c_c(q).wait_send()
            c_r(q).wait_send()

        @pl.when((q >= NA) & (x % 2 == 1))
        def _():
            c_d(q).wait_send()

        @pl.when((q >= NA) & (x == 3))
        def _():
            c_f(q).wait_send()

        @pl.when(j == 0)
        def _():
            c_o(q).wait_send()

        @pl.when(j == 1)
        def _():
            c_b2(q).wait_send()

        return carry

    lax.fori_loop(0, NQ, sent, 0)

    for k in range(5):
        c_stat(0, k, other_core).wait_recv()
    in_top, in_total = stat_in[0, 0:1, :], stat_in[0, 1:2, :]
    m = jnp.maximum(own_top, in_top)
    total = own_total * jnp.exp2(own_top - m) + in_total * jnp.exp2(in_top - m)
    gaps[:ROWS] = (LN2 * (m - positive) + jnp.log(total)).reshape(ROWS)
    for u in range(6):
        ls = slice(u * 128, (u + 1) * 128)
        top, total = mine[u]
        m = top
        for k in range(1, 5):
            m = jnp.maximum(m, stat_in[k, 0:1, ls])
        total = total * jnp.exp2(top - m)
        for k in range(1, 5):
            total = total + stat_in[k, 1:2, ls] * jnp.exp2(stat_in[k, 0:1, ls] - m)
        pc = jnp.sum(posc[u // 2, :, u % 2 * 128:(u % 2 + 1) * 128], axis=0, keepdims=True)
        gaps[ROWS + u * 128:ROWS + (u + 1) * 128] = (LN2 * (m - pc) + jnp.log(total)).reshape(128)

    c_stat(0, 0, other_group).wait_send()
    far_sends(lambda c: c.wait_send())
    near_sends(lambda c: c.wait_send())


def per_device(image_features, text_features, logit_scale, pair_ids):
    vmem = pl.BlockSpec(memory_space=pltpu.VMEM)
    anywhere = pl.BlockSpec(memory_space=pl.ANY)
    out = jax.ShapeDtypeStruct((2 * ROWS,), jnp.float32)
    both = pl.pallas_call(
        kernel,
        out_shape=out,
        in_specs=[anywhere, anywhere, pl.BlockSpec(memory_space=pltpu.HBM), vmem],
        out_specs=vmem,
        scratch_shapes=[
            pltpu.VMEM((ROWS, D), jnp.bfloat16),
            pltpu.VMEM((ROWS, D), jnp.bfloat16),
            pltpu.VMEM((2 * ROWS, D), jnp.bfloat16),
            pltpu.VMEM((5 * ROWS, D), jnp.bfloat16),
            pltpu.VMEM((ROWS, D), jnp.bfloat16),
            pltpu.VMEM((ROWS, D), jnp.bfloat16),
            pltpu.VMEM((2 * ROWS, 128), jnp.float32),
            pltpu.VMEM((2 * ROWS, 128), jnp.float32),
            pltpu.VMEM((30, 8, 128), jnp.float32),
            pltpu.VMEM((30, 8, 128), jnp.float32),
            pltpu.VMEM((ROWS, 128), jnp.float32),
            pltpu.VMEM((3, 8, NT), jnp.float32),
            pltpu.VMEM((ROWS, 128), jnp.float32),
            pltpu.VMEM((1, ROWS), jnp.float32),
            pltpu.VMEM((5, 8, ROWS), jnp.float32),
            pltpu.VMEM((5, 8, ROWS), jnp.float32),
            pltpu.SemaphoreType.DMA((10, NQ)),
            pltpu.SemaphoreType.DMA((7, NQ)),
            pltpu.SemaphoreType.DMA((2, ROWS // PART)),
            pltpu.SemaphoreType.DMA((5,)),
            pltpu.SemaphoreType.DMA((5,)),
            pltpu.SMEM((1,), jnp.float32),
            pltpu.SemaphoreType.DMA,
        ],
        compiler_params=pltpu.CompilerParams(
            collective_id=0, has_side_effects=True, vmem_limit_bytes=56 * 2**20),
        cost_estimate=pl.CostEstimate(flops=15 * 10**9, bytes_accessed=4 * 10**6, transcendentals=12 * 10**6),
    )(image_features, text_features, logit_scale, pair_ids)
    return both[:ROWS], both[ROWS:]


def solution(mesh):
    placed = (P(("group", "blk"), None), P(("group", "blk"), None), P(), P(("group", "blk")))
    return jax.shard_map(
        per_device,
        mesh=mesh,
        in_specs=placed,
        out_specs=(P(("group", "blk")), P(("group", "blk"))),
        check_vma=False,
    )
```
